32 devices in a mesh: plane: 4 (over z), mode: 8 (over y, x, core).
Axes of the slice: x: 2, y: 2, z: 4, core: 2. Of those that a mesh axis runs over, the one named last changes fastest.
Arguments:
- phase_masks: float32 [4, 512, 512], P('plane'), may hold values from -3.140625 to 3.140625
- hg_orders: int32 [32, 2], P('mode'), may hold values from 0 to 44
- spot_index: int32 [32], P('mode'), may hold values from 0 to 1023
Outputs:
- phase_next: float32 [4, 512, 512], P('plane')
The draws below stay inside these ranges and needn't reach their ends.
Inputs may be any that keep to these rules, and one draw needn't show every extreme that they name: `spot_index`: the output spot of each mode; several modes may share a spot.
All inputs are finite; a program needn't handle non-finite values.
Results may differ from the reference program's by a relative error of at most 0.018.
Values may be sent and summed in bfloat16 or wider, within the bound.
A program may use at most 64 MiB of HBM per device.

```python
import math
import jax
import jax.numpy as jnp
from jax import lax

N = 512
ORDERS = 45
SPOT_SIDE = 32
PLANES = 4
MODES = 32
SPOTS = 1024


def place_ends(drawn, stream_key, low, top_value):
    dims = drawn.shape
    spot = [jax.random.randint(jax.random.fold_in(stream_key, axis), (), 0, dims[axis]) for axis in range(len(dims))]
    drawn = drawn.at[tuple(spot)].set(low)
    longest = dims.index(max(dims))
    spot[longest] = (spot[longest] + 1) % dims[longest]
    return drawn.at[tuple(spot)].set(top_value)


def setup_inputs(seed: int = 0) -> dict:
    streams_of = jax.random.split(jax.random.key(seed), 4)
    phase_masks = jnp.clip(jax.random.uniform(streams_of[0], (PLANES, N, N), jnp.float32, -3.140625, 3.140625), -3.140625, 3.140625)
    hg_orders = place_ends(jax.random.randint(streams_of[1], (MODES, 2), 0, ORDERS), jax.random.fold_in(streams_of[1], 1), 0, ORDERS - 1).astype(jnp.int32)
    spot_index = place_ends(jax.random.randint(streams_of[2], (MODES,), 0, SPOTS), jax.random.fold_in(streams_of[2], 1), 0, SPOTS - 1).astype(jnp.int32)
    return {"phase_masks": phase_masks, "hg_orders": hg_orders, "spot_index": spot_index}


CHIRP_RATE = math.pi / 48.0 * (math.pi / 48.0)
AMPLITUDE = 12.0
EPSILON = 1e-06

def kernel_parts(extent):
    positions = jnp.arange(extent, dtype=jnp.int32)
    centred = (positions + extent // 2) % extent - extent // 2
    wrapped = positions[:, None] * positions[None, :] % extent
    chirp_phase = CHIRP_RATE * (centred * centred).astype(jnp.float32)
    angles = 2.0 * math.pi / extent * wrapped.astype(jnp.float32) - chirp_phase[None, :]
    kernel_re = lax.optimization_barrier(jnp.sum(jnp.cos(angles), axis=1)) / extent
    kernel_im = lax.optimization_barrier(jnp.sum(jnp.sin(angles), axis=1)) / extent
    return (kernel_re, kernel_im)

def circulant(values):
    extent = values.shape[0]
    repeated = jnp.tile(values, extent + 1)
    hankel = repeated.reshape(extent, extent + 1)[:, :extent]
    return jnp.roll(jnp.flip(hankel, 1), 1, 1)

def operators(extent):
    kernel_re, kernel_im = kernel_parts(extent)
    matrix_re = circulant(kernel_re)
    matrix_im = circulant(kernel_im)
    prop_re = matrix_re.astype(jnp.bfloat16)
    prop_im = matrix_im.astype(jnp.bfloat16)
    forward_mats = (prop_re, prop_im, (matrix_re + matrix_im).astype(jnp.bfloat16))
    backward_mats = (prop_re, -prop_im, (matrix_re - matrix_im).astype(jnp.bfloat16))
    return (forward_mats, backward_mats)

def left_product(left_re, left_im, left_sum, field_re, field_im):
    field_sum = (field_re.astype(jnp.float32) + field_im.astype(jnp.float32)).astype(jnp.bfloat16)
    first_term = jnp.dot(left_re, field_re, preferred_element_type=jnp.float32)
    second_term = jnp.dot(left_im, field_im, preferred_element_type=jnp.float32)
    third_term = jnp.dot(left_sum, field_sum, preferred_element_type=jnp.float32)
    return (first_term - second_term, third_term - first_term - second_term)

def right_product(field_re, field_im, right_re, right_im, right_sum):
    field_sum = (field_re.astype(jnp.float32) + field_im.astype(jnp.float32)).astype(jnp.bfloat16)
    first_term = jnp.dot(field_re, right_re, preferred_element_type=jnp.float32)
    second_term = jnp.dot(field_im, right_im, preferred_element_type=jnp.float32)
    third_term = jnp.dot(field_sum, right_sum, preferred_element_type=jnp.float32)
    return (first_term - second_term, third_term - first_term - second_term)

def propagate(field_re, field_im, matrices):
    matrix_re, matrix_im, matrix_sum = matrices
    middle_re, middle_im = left_product(matrix_re, matrix_im, matrix_sum, field_re, field_im)
    middle_re, middle_im = lax.optimization_barrier((middle_re.astype(jnp.bfloat16), middle_im.astype(jnp.bfloat16)))
    return right_product(middle_re, middle_im, matrix_re, matrix_im, matrix_sum)

def hermite(orders, extent):
    scaled = (jnp.arange(extent, dtype=jnp.float32) - (extent - 1) / 2.0) / (extent / 48.0)
    lowest = math.pow(math.pi, -0.25) * jnp.exp(-0.5 * scaled * scaled)
    second = math.sqrt(2.0) * scaled * lowest
    chosen = jnp.where((orders == 0)[:, None], lowest[None, :], 0.0)
    chosen = jnp.where((orders == 1)[:, None], second[None, :], chosen)

    def advance(degree, carried):
        previous, current, picked = carried
        degree_f = degree.astype(jnp.float32)
        higher = jnp.sqrt(2.0 / (degree_f + 1.0)) * scaled * current - jnp.sqrt(degree_f / (degree_f + 1.0)) * previous
        picked = jnp.where((orders == degree + 1)[:, None], higher[None, :], picked)
        return (current, higher, picked)
    previous, current, chosen = lax.fori_loop(1, ORDERS - 1, advance, (lowest, second, chosen))
    return chosen

def spot_profile(spots, extent):
    coords = jnp.arange(extent, dtype=jnp.float32) - (extent - 1) / 2.0
    spacing = extent / 40.0
    spot_width = extent / 120.0
    centre = (SPOT_SIDE - 1) / 2.0
    spot_row = (spots // SPOT_SIDE).astype(jnp.float32) - centre
    spot_col = (spots % SPOT_SIDE).astype(jnp.float32) - centre
    offset_x = (coords[None, :] - spacing * spot_row[:, None]) / spot_width
    offset_y = (coords[None, :] - spacing * spot_col[:, None]) / spot_width
    return (jnp.exp(-offset_x * offset_x), jnp.exp(-offset_y * offset_y))

def mode_tables(orders, spots, extent):
    profile_x, profile_y = spot_profile(spots, extent)
    return (AMPLITUDE * hermite(orders[:, 0], extent), hermite(orders[:, 1], extent), profile_x, profile_y)

def apply_mask(field_re, field_im, cos_mask, sin_mask):
    masked_re = (field_re * cos_mask - field_im * sin_mask).astype(jnp.bfloat16)
    masked_im = (field_re * sin_mask + field_im * cos_mask).astype(jnp.bfloat16)
    return lax.optimization_barrier((masked_re, masked_im))

def remove_mask(back_re, back_im, cos_mask, sin_mask):
    reply_re = (back_re * cos_mask + back_im * sin_mask).astype(jnp.bfloat16)
    reply_im = (back_im * cos_mask - back_re * sin_mask).astype(jnp.bfloat16)
    return lax.optimization_barrier((reply_re, reply_im))

def whole_mode(input_x, input_y, target, cos_masks, sin_masks, forward_mats, backward_mats):
    plane_count = cos_masks.shape[0]
    field_re = input_x[:, None] * input_y[None, :]
    field_im = jnp.zeros_like(field_re)
    masked_fields = []
    for plane_at in range(plane_count):
        masked_re, masked_im = apply_mask(field_re, field_im, cos_masks[plane_at], sin_masks[plane_at])
        masked_fields.append((masked_re, masked_im))
        out_re, out_im = propagate(masked_re, masked_im, forward_mats)
        rounded = lax.optimization_barrier((out_re.astype(jnp.bfloat16), out_im.astype(jnp.bfloat16)))
        field_re = rounded[0].astype(jnp.float32)
        field_im = rounded[1].astype(jnp.float32)
    coupling_re = jnp.sum(target * out_re)
    coupling_im = jnp.sum(target * out_im)
    source_re, source_im = lax.optimization_barrier(((coupling_re * target).astype(jnp.bfloat16), (coupling_im * target).astype(jnp.bfloat16)))
    grad_terms = []
    for plane_at in reversed(range(plane_count)):
        back_re, back_im = propagate(source_re, source_im, backward_mats)
        masked_re, masked_im = masked_fields[plane_at]
        grad_terms.append(2.0 * (back_im * masked_re.astype(jnp.float32) - back_re * masked_im.astype(jnp.float32)))
        source_re, source_im = remove_mask(back_re, back_im, cos_masks[plane_at], sin_masks[plane_at])
    return jnp.stack(grad_terms[::-1])

def reference(phase_masks, hg_orders, spot_index):
    extent = phase_masks.shape[1]
    plane_count = phase_masks.shape[0]
    forward_mats, backward_mats = operators(extent)
    cos_masks = jnp.cos(phase_masks)
    sin_masks = jnp.sin(phase_masks)
    tables = mode_tables(hg_orders, spot_index, extent)

    def one_mode(grad_total, entries):
        input_x, input_y, profile_x, profile_y = entries
        target = profile_x[:, None] * profile_y[None, :]
        return (grad_total + whole_mode(input_x, input_y, target, cos_masks, sin_masks, forward_mats, backward_mats), None)
    grad_total, unused = lax.scan(one_mode, jnp.zeros((plane_count, extent, extent), jnp.float32), tables)
    mean_square = lax.optimization_barrier(jnp.mean(grad_total * grad_total, axis=(1, 2), keepdims=True))
    return phase_masks + grad_total / jnp.sqrt(mean_square + EPSILON)
```

```python
import functools
import math

import jax
import jax.numpy as jnp
from jax import lax
from jax.experimental import pallas as pl
from jax.experimental.pallas import tpu as pltpu
from jax.sharding import PartitionSpec as P

ORDERS = 45
SPOT_SIDE = 32
CHIRP_RATE = math.pi / 48.0 * (math.pi / 48.0)
AMPLITUDE = 12.0
EPSILON = 1e-06
CODE = 26.0
CHUNK = 16
F32 = jnp.float32
BF16 = jnp.bfloat16
MESH = pl.DeviceIdType.MESH

SIN_HALF = [(-1.0) ** n / math.factorial(2 * n + 1) for n in range(6)]
COS_HALF = [(-1.0) ** n / math.factorial(2 * n) for n in range(6)]


def horner(u, coefficients):
    total = jnp.full_like(u, coefficients[-1])
    for value in coefficients[-2::-1]:
        total = total * u + value
    return total


def sincos(x):
    h = 0.5 * x
    u = h * h
    s = h * horner(u, SIN_HALF)
    c = horner(u, COS_HALF)
    return 2.0 * s * c, 1.0 - 2.0 * s * s


def exact_dot(a, b, contract):
    return lax.dot_general(
        a, b, ((contract[:1], contract[1:]), ((), ())),
        precision=lax.Precision.HIGHEST, preferred_element_type=F32,
    )


def make_operators(n, left_ref, right_ref, prop_ref):
    h = n // 2
    rows = lax.broadcasted_iota(jnp.int32, (h, h), 0)
    slots = lax.broadcasted_iota(jnp.int32, (h, h), 1)
    for a in range(2):
        freq = 2 * slots + a
        turn = ((freq * rows + h) & (n - 1)) - h
        s, c = sincos(turn.astype(F32) * (2.0 * math.pi / n))
        basis = jnp.concatenate([c, s], axis=1)
        freq_row = 2 * lax.broadcasted_iota(jnp.int32, (8, h), 1) + a
        centred = ((freq_row + h) & (n - 1)) - h
        turns = (centred * centred).astype(F32) * (CHIRP_RATE / (2.0 * math.pi))
        turns = turns - jnp.floor(turns + 0.5)
        chirp_s, chirp_c = sincos(turns * (2.0 * math.pi))
        for part, weight in enumerate((chirp_c, -chirp_s)):
            weight = weight[:1] * (1.0 / n)
            weighted = basis * jnp.concatenate([weight, weight], axis=1)
            prop_ref[a, part] = exact_dot(weighted, basis, (1, 1))
        re, im = prop_ref[a, 0].astype(BF16), prop_ref[a, 1].astype(BF16)
        left_ref[a, :h, :h] = re
        left_ref[a, :h, h:] = -im
        left_ref[a, h:, :h] = im
        left_ref[a, h:, h:] = re
        right_ref[a, :h, :h] = re
        right_ref[a, :h, h:] = im
        right_ref[a, h:, :h] = -im
        right_ref[a, h:, h:] = re


def make_tables(n, order_x, order_y, spot, prop_ref, row_ref, col_ref):
    h = n // 2
    coords = lax.broadcasted_iota(jnp.int32, (8, n), 1).astype(F32) - (n - 1) / 2.0
    row_id = lax.broadcasted_iota(jnp.int32, (8, n), 0)
    orders = jnp.where(row_id == 0, order_x, order_y)
    scaled = coords * (48.0 / n)
    previous = math.pow(math.pi, -0.25) * jnp.exp(-0.5 * scaled * scaled)
    current = math.sqrt(2.0) * scaled * previous
    picked = jnp.where(orders == 0, previous, current)
    for degree in range(1, ORDERS - 1):
        higher = (
            math.sqrt(2.0 / (degree + 1.0)) * scaled * current
            - math.sqrt(degree / (degree + 1.0)) * previous
        )
        picked = jnp.where(orders == degree + 1, higher, picked)
        previous, current = current, higher
    centre = (SPOT_SIDE - 1) / 2.0
    spot_row = (spot // SPOT_SIDE).astype(F32) - centre
    spot_col = (spot % SPOT_SIDE).astype(F32) - centre
    place = jnp.where(row_id == 0, spot_row, spot_col)
    offset = (coords - (n / 40.0) * place) * (120.0 / n)
    profile = jnp.exp(-offset * offset)
    spread = []
    for part in range(2):
        s = exact_dot(profile[:, :h] + profile[:, h:], prop_ref[0, part], (1, 0))
        d = exact_dot(profile[:, :h] - profile[:, h:], prop_ref[1, part], (1, 0))
        spread.append(jnp.concatenate([s + d, s - d], axis=1))
    table = jnp.concatenate(
        [
            AMPLITUDE * picked[0:1], picked[1:2],
            spread[0][0:1], spread[1][0:1], spread[0][1:2], spread[1][1:2],
            jnp.zeros((2, n), F32),
        ],
        axis=0,
    )
    row_ref[...] = table
    wide = jnp.concatenate([table, jnp.zeros((120, n), F32)], axis=0)
    col_ref[...] = wide.T


def kernel(
    planes, modes, orders_ref, spots_ref, mask_ref, out_ref,
    code, cosm, sinm, g_re, g_im, x_buf, w_buf, y_buf, left, right, prop, row_tab, col_tab,
    grad, in_a, sum_a, in_b, piece, in_c, final,
    mz_s, mz_r, ml_s, ml_r, mc_s, mc_r, a_s, a_r, b_s, b_r, c_s, c_r, d_s, d_r, e_s, e_r,
):
    n = mask_ref.shape[-1]
    h = n // 2
    chips = modes // 2
    rows = n // chips
    p = lax.axis_index("plane")
    m = lax.axis_index("mode")
    core = m % 2
    chip = m // 2
    partner = m + 1 - 2 * core

    def at_chip(step):
        return (chip + step) % chips

    def rows_of(which):
        return pl.ds(pl.multiple_of(which * rows, rows), rows)

    def remote(src, dst, send, recv, plane=None, mode=None):
        return pltpu.make_async_remote_copy(
            src_ref=src, dst_ref=dst, send_sem=send, recv_sem=recv,
            device_id=(p if plane is None else plane, m if mode is None else mode),
            device_id_type=MESH,
        )

    mine = rows_of(chip)

    def mask_z(step):
        spot = code.at[p, core, mine]
        return remote(spot, spot, mz_s.at[step - 1], mz_r.at[p], plane=(p + step) % planes)

    def mask_z_in(k):
        spot = code.at[k, core, mine]
        return remote(spot, spot, mz_s.at[0], mz_r.at[k], plane=(p + 1) % planes)

    def mask_layer(k, step):
        spot = code.at[k, core, mine]
        return remote(
            spot, spot, ml_s.at[k, step - 1], ml_r.at[k, step - 1], mode=at_chip(step) * 2 + core
        )

    def mask_core(k):
        return remote(code.at[k, core], code.at[k, core], mc_s.at[k], mc_r.at[k], mode=partner)

    def grad_a(k):
        return remote(grad.at[k, 1 - core], in_a.at[k], a_s.at[k], a_r.at[k], mode=partner)

    def grad_b(k, step):
        there = at_chip(step)
        return remote(
            sum_a.at[k, rows_of(there)], in_b.at[k, step - 1], b_s.at[k, step - 1],
            b_r.at[k, step - 1], mode=there * 2 + core,
        )

    def grad_c(k):
        return remote(piece.at[k], in_c.at[p], c_s.at[k], c_r.at[p], plane=k)

    def grad_c_in(source):
        return remote(piece.at[0], in_c.at[source], c_s.at[0], c_r.at[source], plane=source)

    def grad_d(step):
        spot = final.at[core, mine]
        return remote(
            spot, spot, d_s.at[step - 1], d_r.at[step - 1], mode=at_chip(step) * 2 + core
        )

    def grad_e():
        return remote(final.at[core], final.at[core], e_s.at[0], e_r.at[0], mode=partner)

    barrier = pltpu.get_barrier_semaphore()
    for step in range(1, planes):
        pl.semaphore_signal(
            barrier, inc=1, device_id=((p + step) % planes, m), device_id_type=MESH
        )
    for step in range(1, chips):
        pl.semaphore_signal(
            barrier, inc=1, device_id=(p, at_chip(step) * 2 + core), device_id_type=MESH
        )
    pl.semaphore_signal(barrier, inc=1, device_id=(p, partner), device_id_type=MESH)

    for b in range(2):
        code[p, b] = jnp.exp(CODE * mask_ref[0, :, b * h : (b + 1) * h]).astype(BF16)
    pl.semaphore_wait(barrier, planes - 1 + chips - 1 + 1)

    for step in range(1, planes):
        mask_z(step).start()

    make_operators(n, left, right, prop)

    for k in range(planes):
        @pl.when(p != k)
        def _():
            mask_z_in(k).wait_recv()
            for step in range(1, chips):
                mask_layer(k, step).start()

    make_tables(n, orders_ref[p, 0], orders_ref[p, 1], spots_ref[p], prop, row_tab, col_tab)

    quads = [(a, b) for a in range(2) for b in range(2)]

    def span(i, a):
        return pl.ds(pl.multiple_of(a * h + i * CHUNK, CHUNK), CHUNK)

    def hadamard(q):
        top, bottom = q[0, 0] + q[0, 1], q[1, 0] + q[1, 1]
        top_d, bottom_d = q[0, 0] - q[0, 1], q[1, 0] - q[1, 1]
        return {
            (0, 0): top + bottom, (0, 1): top_d + bottom_d,
            (1, 0): top - bottom, (1, 1): top_d - bottom_d,
        }

    def combined(i):
        re = hadamard({(a, b): y_buf[b, span(i, a), :h] for a, b in quads})
        im = hadamard({(a, b): y_buf[b, span(i, a), h:] for a, b in quads})
        return re, im

    def put_sums(i, re, im):
        for part, q in enumerate((hadamard(re), hadamard(im))):
            for a, b in quads:
                x_buf[a, span(i, part), b * h : (b + 1) * h] = q[a, b].astype(BF16)

    def products(first, second):
        for a in range(2):
            v = jnp.dot(first[a], x_buf[a], preferred_element_type=F32)
            for b in range(2):
                for part in range(2):
                    w_buf[b, a * h : (a + 1) * h, part * h : (part + 1) * h] = v[
                        part * h : (part + 1) * h, b * h : (b + 1) * h
                    ].astype(BF16)
        for b in range(2):
            y_buf[b] = jnp.dot(w_buf[b], second[b], preferred_element_type=F32)

    def outer(i, a, b):
        ar, ai = col_tab[span(i, a), 2:3], col_tab[span(i, a), 3:4]
        br, bi = row_tab[4:5, b * h : (b + 1) * h], row_tab[5:6, b * h : (b + 1) * h]
        return ar * br - ai * bi, ar * bi + ai * br

    for k in range(planes):
        @pl.when(p != k)
        def _():
            for step in range(1, chips):
                mask_layer(k, step).wait_recv()
            mask_core(k).start()
            mask_core(k).wait_recv()

        last = k == planes - 1

        def forward(i, carry):
            if k == 0:
                field_re = {
                    (a, b): col_tab[span(i, a), 0:1] * row_tab[1:2, b * h : (b + 1) * h]
                    for a, b in quads
                }
                field_im = None
            else:
                field_re, field_im = combined(i)
            masked_re, masked_im = {}, {}
            for a, b in quads:
                phase = jnp.log(code[k, b, span(i, a)].astype(F32)) * (1.0 / CODE)
                s, c = sincos(phase)
                cosm[k, b, span(i, a)] = c
                sinm[k, b, span(i, a)] = s
                if field_im is None:
                    re, im = field_re[a, b] * c, field_re[a, b] * s
                else:
                    fr, fi = field_re[a, b], field_im[a, b]
                    re, im = fr * c - fi * s, fr * s + fi * c
                masked_re[a, b], masked_im[a, b] = re, im
                g_re[k, b, span(i, a)] = re.astype(BF16)
                g_im[k, b, span(i, a)] = im.astype(BF16)
            if not last:
                put_sums(i, masked_re, masked_im)
                return carry
            total_re, total_im = carry
            for a, b in quads:
                er, ei = outer(i, a, b)
                re, im = masked_re[a, b], masked_im[a, b]
                total_re += er * re - ei * im
                total_im += er * im + ei * re
            return total_re, total_im

        zero = jnp.zeros((CHUNK, h), F32)
        totals = lax.fori_loop(0, h // CHUNK, forward, (zero, zero) if last else 0)
        if not last:
            products(left, right)
    coupling_re = jnp.sum(totals[0], keepdims=True)
    coupling_im = jnp.sum(totals[1], keepdims=True)

    def settle_a(k):
        grad_a(k).wait_recv()
        sum_a[k] = (grad[k, core].astype(F32) + in_a[k].astype(F32)).astype(BF16)
        for step in range(1, chips):
            grad_b(k, step).start()

    def settle_b(k):
        for step in range(1, chips):
            grad_b(k, step).wait_recv()
        total = sum_a[k, mine].astype(F32)
        for step in range(1, chips):
            total += in_b[k, step - 1].astype(F32)
        piece[k] = total.astype(BF16)

        @pl.when(p != k)
        def _():
            grad_c(k).start()

        @pl.when(p == k)
        def _():
            in_c[k] = piece[k]

    for k in range(planes - 1, -1, -1):
        def backward(i, carry):
            if k == planes - 1:
                back_re, back_im = {}, {}
                for a, b in quads:
                    er, ei = outer(i, a, b)
                    back_re[a, b] = coupling_re * er + coupling_im * ei
                    back_im[a, b] = coupling_im * er - coupling_re * ei
            else:
                back_re, back_im = combined(i)
            reply_re, reply_im = {}, {}
            for a, b in quads:
                br, bi = back_re[a, b], back_im[a, b]
                gr = g_re[k, b, span(i, a)].astype(F32)
                gi = g_im[k, b, span(i, a)].astype(F32)
                grad[k, b, span(i, a)] = (2.0 * (bi * gr - br * gi)).astype(BF16)
                if k > 0:
                    c, s = cosm[k, b, span(i, a)], sinm[k, b, span(i, a)]
                    reply_re[a, b] = br * c + bi * s
                    reply_im[a, b] = bi * c - br * s
            if k > 0:
                put_sums(i, reply_re, reply_im)
            return carry

        lax.fori_loop(0, h // CHUNK, backward, 0)
        grad_a(k).start()
        if k + 2 < planes:
            settle_b(k + 2)
        if k + 1 < planes:
            settle_a(k + 1)
        if k > 0:
            products(right, left)
    settle_a(0)
    if planes > 1:
        settle_b(1)
    settle_b(0)

    for k in range(planes):
        @pl.when(p != k)
        def _():
            grad_c_in(k).wait_recv()
    total = in_c[0].astype(F32)
    for k in range(1, planes):
        total += in_c[k].astype(F32)
    final[core, mine] = total.astype(BF16)
    for step in range(1, chips):
        grad_d(step).start()
    for step in range(1, chips):
        grad_d(step).wait_recv()
    grad_e().start()
    grad_e().wait_recv()

    def square(i, carry):
        here = pl.ds(pl.multiple_of(i * CHUNK, CHUNK), CHUNK)
        for b in range(2):
            g = final[b, here].astype(F32)
            carry += g * g
        return carry

    squares = lax.fori_loop(0, n // CHUNK, square, jnp.zeros((CHUNK, h), F32))
    mean_square = jnp.sum(squares, keepdims=True) * (1.0 / (n * n))
    scale = 1.0 / jnp.sqrt(mean_square + EPSILON)

    def finish(i, carry):
        here = pl.ds(pl.multiple_of(i * CHUNK, CHUNK), CHUNK)
        for b in range(2):
            cols = slice(b * h, (b + 1) * h)
            out_ref[0, here, cols] = mask_ref[0, here, cols] + final[b, here].astype(F32) * scale
        return carry

    lax.fori_loop(0, n // CHUNK, finish, 0)

    for step in range(1, planes):
        mask_z(step).wait_send()
    for k in range(planes):
        @pl.when(p != k)
        def _():
            for step in range(1, chips):
                mask_layer(k, step).wait_send()
            mask_core(k).wait_send()
            grad_c(k).wait_send()

        grad_a(k).wait_send()
        for step in range(1, chips):
            grad_b(k, step).wait_send()
    for step in range(1, chips):
        grad_d(step).wait_send()
    grad_e().wait_send()


def shards(planes, modes, phase_masks, hg_orders, spot_index):
    n = phase_masks.shape[1]
    h = n // 2
    chips = modes // 2
    rows = n // chips
    others = max(chips - 1, 1)
    assert hg_orders.shape[0] == planes and n & (n - 1) == 0
    dma = pltpu.SemaphoreType.DMA
    vmem = pltpu.VMEM
    return pl.pallas_call(
        functools.partial(kernel, planes, modes),
        out_shape=jax.ShapeDtypeStruct((1, n, n), F32),
        in_specs=[
            pl.BlockSpec(memory_space=pltpu.SMEM),
            pl.BlockSpec(memory_space=pltpu.SMEM),
            pl.BlockSpec(memory_space=pltpu.VMEM),
        ],
        out_specs=pl.BlockSpec(memory_space=pltpu.VMEM),
        scratch_shapes=[
            vmem((planes, 2, n, h), BF16),
            vmem((planes, 2, n, h), F32),
            vmem((planes, 2, n, h), F32),
            vmem((planes, 2, n, h), BF16),
            vmem((planes, 2, n, h), BF16),
            vmem((2, n, n), BF16),
            vmem((2, n, n), BF16),
            vmem((2, n, n), F32),
            vmem((2, n, n), BF16),
            vmem((2, n, n), BF16),
            vmem((2, 2, h, h), F32),
            vmem((8, n), F32),
            vmem((n, 128), F32),
            vmem((planes, 2, n, h), BF16),
            vmem((planes, n, h), BF16),
            vmem((planes, n, h), BF16),
            vmem((planes, others, rows, h), BF16),
            vmem((planes, rows, h), BF16),
            vmem((planes, rows, h), BF16),
            vmem((2, n, h), BF16),
            dma((max(planes - 1, 1),)), dma((planes,)),
            dma((planes, others)), dma((planes, others)),
            dma((planes,)), dma((planes,)),
            dma((planes,)), dma((planes,)),
            dma((planes, others)), dma((planes, others)),
            dma((planes,)), dma((planes,)),
            dma((others,)), dma((others,)),
            dma((1,)), dma((1,)),
        ],
        compiler_params=pltpu.CompilerParams(
            collective_id=0, has_side_effects=True, vmem_limit_bytes=52 * 1024 * 1024
        ),
        name="phase_update",
    )(hg_orders, spot_index, phase_masks)


def solution(mesh):
    planes, modes = mesh.shape["plane"], mesh.shape["mode"]
    return jax.shard_map(
        functools.partial(shards, planes, modes),
        mesh=mesh,
        in_specs=(P("plane", None, None), P("mode", None), P("mode")),
        out_specs=P("plane", None, None),
        check_vma=False,
    )
```

```python
import functools
import math

import jax
import jax.numpy as jnp
from jax import lax
from jax.experimental import pallas as pl
from jax.experimental.pallas import tpu as pltpu
from jax.sharding import PartitionSpec as P

ORDERS = 45
SPOT_SIDE = 32
CHIRP_RATE = math.pi / 48.0 * (math.pi / 48.0)
AMPLITUDE = 12.0
EPSILON = 1e-06
CODE = 26.0
CHUNK = 16
F32 = jnp.float32
BF16 = jnp.bfloat16
MESH = pl.DeviceIdType.MESH

SIN_HALF = [(-1.0) ** n / math.factorial(2 * n + 1) for n in range(6)]
COS_HALF = [(-1.0) ** n / math.factorial(2 * n) for n in range(6)]


def horner(u, coefficients):
    total = jnp.full_like(u, coefficients[-1])
    for value in coefficients[-2::-1]:
        total = total * u + value
    return total


def sincos(x):
    h = 0.5 * x
    u = h * h
    s = h * horner(u, SIN_HALF)
    c = horner(u, COS_HALF)
    return 2.0 * s * c, 1.0 - 2.0 * s * s


def exact_dot(a, b, contract):
    return lax.dot_general(
        a, b, ((contract[:1], contract[1:]), ((), ())),
        precision=lax.Precision.HIGHEST, preferred_element_type=F32,
    )


def make_operators(n, left_ref, right_ref, prop_ref):
    h = n // 2
    rows = lax.broadcasted_iota(jnp.int32, (h, h), 0)
    slots = lax.broadcasted_iota(jnp.int32, (h, h), 1)
    for a in range(2):
        freq = 2 * slots + a
        turn = ((freq * rows + h) & (n - 1)) - h
        s, c = sincos(turn.astype(F32) * (2.0 * math.pi / n))
        basis = jnp.concatenate([c, s], axis=1)
        freq_row = 2 * lax.broadcasted_iota(jnp.int32, (8, h), 1) + a
        centred = ((freq_row + h) & (n - 1)) - h
        turns = (centred * centred).astype(F32) * (CHIRP_RATE / (2.0 * math.pi))
        turns = turns - jnp.floor(turns + 0.5)
        chirp_s, chirp_c = sincos(turns * (2.0 * math.pi))
        for part, weight in enumerate((chirp_c, -chirp_s)):
            weight = weight[:1] * (1.0 / n)
            weighted = basis * jnp.concatenate([weight, weight], axis=1)
            prop_ref[a, part] = exact_dot(weighted, basis, (1, 1))
        re, im = prop_ref[a, 0].astype(BF16), prop_ref[a, 1].astype(BF16)
        left_ref[a, :h, :h] = re
        left_ref[a, :h, h:] = -im
        left_ref[a, h:, :h] = im
        left_ref[a, h:, h:] = re
        right_ref[a, :h, :h] = re
        right_ref[a, :h, h:] = im
        right_ref[a, h:, :h] = -im
        right_ref[a, h:, h:] = re


def make_tables(n, order_x, order_y, spot, prop_ref, row_ref, col_ref):
    h = n // 2
    coords = lax.broadcasted_iota(jnp.int32, (8, n), 1).astype(F32) - (n - 1) / 2.0
    row_id = lax.broadcasted_iota(jnp.int32, (8, n), 0)
    orders = jnp.where(row_id == 0, order_x, order_y)
    scaled = coords * (48.0 / n)
    previous = math.pow(math.pi, -0.25) * jnp.exp(-0.5 * scaled * scaled)
    current = math.sqrt(2.0) * scaled * previous
    picked = jnp.where(orders == 0, previous, current)
    for degree in range(1, ORDERS - 1):
        higher = (
            math.sqrt(2.0 / (degree + 1.0)) * scaled * current
            - math.sqrt(degree / (degree + 1.0)) * previous
        )
        picked = jnp.where(orders == degree + 1, higher, picked)
        previous, current = current, higher
    centre = (SPOT_SIDE - 1) / 2.0
    spot_row = (spot // SPOT_SIDE).astype(F32) - centre
    spot_col = (spot % SPOT_SIDE).astype(F32) - centre
    place = jnp.where(row_id == 0, spot_row, spot_col)
    offset = (coords - (n / 40.0) * place) * (120.0 / n)
    profile = jnp.exp(-offset * offset)
    spread = []
    for part in range(2):
        s = exact_dot(profile[:, :h] + profile[:, h:], prop_ref[0, part], (1, 0))
        d = exact_dot(profile[:, :h] - profile[:, h:], prop_ref[1, part], (1, 0))
        spread.append(jnp.concatenate([s + d, s - d], axis=1))
    table = jnp.concatenate(
        [
            AMPLITUDE * picked[0:1], picked[1:2],
            spread[0][0:1], spread[1][0:1], spread[0][1:2], spread[1][1:2],
            jnp.zeros((2, n), F32),
        ],
        axis=0,
    )
    row_ref[...] = table
    wide = jnp.concatenate([table, jnp.zeros((120, n), F32)], axis=0)
    col_ref[...] = wide.T


def kernel(
    planes, modes, orders_ref, spots_ref, mask_ref, out_ref,
    code, cosm, sinm, g_re, g_im, x_buf, w_buf, y_buf, left, right, prop, row_tab, col_tab,
    grad, in_a, sum_a, in_b, piece, in_c, final,
    mz_s, mz_r, ml_s, ml_r, mc_s, mc_r, a_s, a_r, b_s, b_r, c_s, c_r, d_s, d_r, e_s, e_r,
):
    n = mask_ref.shape[-1]
    h = n // 2
    chips = modes // 2
    rows = n // chips
    p = lax.axis_index("plane")
    m = lax.axis_index("mode")
    core = m % 2
    chip = m // 2
    partner = m + 1 - 2 * core

    def at_chip(step):
        return (chip + step) % chips

    def rows_of(which):
        return pl.ds(pl.multiple_of(which * rows, rows), rows)

    def remote(src, dst, send, recv, plane=None, mode=None):
        return pltpu.make_async_remote_copy(
            src_ref=src, dst_ref=dst, send_sem=send, recv_sem=recv,
            device_id=(p if plane is None else plane, m if mode is None else mode),
            device_id_type=MESH,
        )

    mine = rows_of(chip)

    def mask_z(step):
        spot = code.at[p, core, mine]
        return remote(spot, spot, mz_s.at[step - 1], mz_r.at[p], plane=(p + step) % planes)

    def mask_z_in(k):
        spot = code.at[k, core, mine]
        return remote(spot, spot, mz_s.at[0], mz_r.at[k], plane=(p + 1) % planes)

    def mask_layer(k, step):
        spot = code.at[k, core, mine]
        return remote(
            spot, spot, ml_s.at[k, step - 1], ml_r.at[k, step - 1], mode=at_chip(step) * 2 + core
        )

    def mask_core(k):
        return remote(code.at[k, core], code.at[k, core], mc_s.at[k], mc_r.at[k], mode=partner)

    def grad_a(k):
        return remote(grad.at[k, 1 - core], in_a.at[k], a_s.at[k], a_r.at[k], mode=partner)

    def grad_b(k, step):
        there = at_chip(step)
        return remote(
            sum_a.at[k, rows_of(there)], in_b.at[k, step - 1], b_s.at[k, step - 1],
            b_r.at[k, step - 1], mode=there * 2 + core,
        )

    def grad_c(k):
        return remote(piece.at[k], in_c.at[p], c_s.at[k], c_r.at[p], plane=k)

    def grad_c_in(source):
        return remote(piece.at[0], in_c.at[source], c_s.at[0], c_r.at[source], plane=source)

    def grad_d(step):
        spot = final.at[core, mine]
        return remote(
            spot, spot, d_s.at[step - 1], d_r.at[step - 1], mode=at_chip(step) * 2 + core
        )

    def grad_e(step):
        spot = final.at[core, rows_of(at_chip(chips - step))]
        return remote(spot, spot, e_s.at[step], e_r.at[step], mode=partner)

    barrier = pltpu.get_barrier_semaphore()
    for step in range(1, planes):
        pl.semaphore_signal(
            barrier, inc=1, device_id=((p + step) % planes, m), device_id_type=MESH
        )
    for step in range(1, chips):
        pl.semaphore_signal(
            barrier, inc=1, device_id=(p, at_chip(step) * 2 + core), device_id_type=MESH
        )
    pl.semaphore_signal(barrier, inc=1, device_id=(p, partner), device_id_type=MESH)

    for b in range(2):
        code[p, b] = jnp.exp(CODE * mask_ref[0, :, b * h : (b + 1) * h]).astype(BF16)
    pl.semaphore_wait(barrier, planes - 1 + chips - 1 + 1)

    for step in range(1, planes):
        mask_z(step).start()

    make_operators(n, left, right, prop)

    def spread_layer(k):
        @pl.when(p != k)
        def _():
            mask_z_in(k).wait_recv()
            for step in range(1, chips):
                mask_layer(k, step).start()

    def spread_core(k):
        @pl.when(p != k)
        def _():
            for step in range(1, chips):
                mask_layer(k, step).wait_recv()
            mask_core(k).start()

    for k in range(min(2, planes)):
        spread_layer(k)

    make_tables(
        n, orders_ref[0, p], orders_ref[1, p], spots_ref[p], prop, row_tab, col_tab
    )
    spread_core(0)

    quads = [(a, b) for a in range(2) for b in range(2)]

    def span(i, a):
        return pl.ds(pl.multiple_of(a * h + i * CHUNK, CHUNK), CHUNK)

    def hadamard(q):
        top, bottom = q[0, 0] + q[0, 1], q[1, 0] + q[1, 1]
        top_d, bottom_d = q[0, 0] - q[0, 1], q[1, 0] - q[1, 1]
        return {
            (0, 0): top + bottom, (0, 1): top_d + bottom_d,
            (1, 0): top - bottom, (1, 1): top_d - bottom_d,
        }

    def combined(i):
        re = hadamard({(a, b): y_buf[b, span(i, a), :h] for a, b in quads})
        im = hadamard({(a, b): y_buf[b, span(i, a), h:] for a, b in quads})
        return re, im

    def put_sums(i, re, im):
        for part, q in enumerate((hadamard(re), hadamard(im))):
            for a, b in quads:
                x_buf[a, span(i, part), b * h : (b + 1) * h] = q[a, b].astype(BF16)

    def products(first, second):
        for a in range(2):
            v = jnp.dot(first[a], x_buf[a], preferred_element_type=F32)
            for b in range(2):
                for part in range(2):
                    w_buf[b, a * h : (a + 1) * h, part * h : (part + 1) * h] = v[
                        part * h : (part + 1) * h, b * h : (b + 1) * h
                    ].astype(BF16)
        for b in range(2):
            y_buf[b] = jnp.dot(w_buf[b], second[b], preferred_element_type=F32)

    def outer(i, a, b):
        ar, ai = col_tab[span(i, a), 2:3], col_tab[span(i, a), 3:4]
        br, bi = row_tab[4:5, b * h : (b + 1) * h], row_tab[5:6, b * h : (b + 1) * h]
        return ar * br - ai * bi, ar * bi + ai * br

    for k in range(planes):
        @pl.when(p != k)
        def _():
            mask_core(k).wait_recv()

        if k + 2 < planes:
            spread_layer(k + 2)
        last = k == planes - 1

        def forward(i, carry):
            if k == 0:
                field_re = {
                    (a, b): col_tab[span(i, a), 0:1] * row_tab[1:2, b * h : (b + 1) * h]
                    for a, b in quads
                }
                field_im = None
            else:
                field_re, field_im = combined(i)
            masked_re, masked_im = {}, {}
            for a, b in quads:
                phase = jnp.log(code[k, b, span(i, a)].astype(F32)) * (1.0 / CODE)
                s, c = sincos(phase)
                cosm[k, b, span(i, a)] = c
                sinm[k, b, span(i, a)] = s
                if field_im is None:
                    re, im = field_re[a, b] * c, field_re[a, b] * s
                else:
                    fr, fi = field_re[a, b], field_im[a, b]
                    re, im = fr * c - fi * s, fr * s + fi * c
                masked_re[a, b], masked_im[a, b] = re, im
                g_re[k, b, span(i, a)] = re.astype(BF16)
                g_im[k, b, span(i, a)] = im.astype(BF16)
            if not last:
                put_sums(i, masked_re, masked_im)
                return carry
            total_re, total_im = carry
            for a, b in quads:
                er, ei = outer(i, a, b)
                re, im = masked_re[a, b], masked_im[a, b]
                total_re += er * re - ei * im
                total_im += er * im + ei * re
            return total_re, total_im

        zero = jnp.zeros((CHUNK, h), F32)
        totals = lax.fori_loop(0, h // CHUNK, forward, (zero, zero) if last else 0)
        if not last:
            spread_core(k + 1)
            products(left, right)
    coupling_re = jnp.sum(totals[0], keepdims=True)
    coupling_im = jnp.sum(totals[1], keepdims=True)

    def settle_a(k):
        grad_a(k).wait_recv()
        sum_a[k] = (grad[k, core].astype(F32) + in_a[k].astype(F32)).astype(BF16)
        for step in range(1, chips):
            grad_b(k, step).start()

    def settle_b(k):
        for step in range(1, chips):
            grad_b(k, step).wait_recv()
        total = sum_a[k, mine].astype(F32)
        for step in range(1, chips):
            total += in_b[k, step - 1].astype(F32)
        piece[k] = total.astype(BF16)

        @pl.when(p != k)
        def _():
            grad_c(k).start()

        @pl.when(p == k)
        def _():
            in_c[k] = piece[k]

    for k in range(planes - 1, -1, -1):
        def backward(i, carry):
            if k == planes - 1:
                back_re, back_im = {}, {}
                for a, b in quads:
                    er, ei = outer(i, a, b)
                    back_re[a, b] = coupling_re * er + coupling_im * ei
                    back_im[a, b] = coupling_im * er - coupling_re * ei
            else:
                back_re, back_im = combined(i)
            reply_re, reply_im = {}, {}
            for a, b in quads:
                br, bi = back_re[a, b], back_im[a, b]
                gr = g_re[k, b, span(i, a)].astype(F32)
                gi = g_im[k, b, span(i, a)].astype(F32)
                grad[k, b, span(i, a)] = (2.0 * (bi * gr - br * gi)).astype(BF16)
                if k > 0:
                    c, s = cosm[k, b, span(i, a)], sinm[k, b, span(i, a)]
                    reply_re[a, b] = br * c + bi * s
                    reply_im[a, b] = bi * c - br * s
            if k > 0:
                put_sums(i, reply_re, reply_im)
            return carry

        lax.fori_loop(0, h // CHUNK, backward, 0)
        grad_a(k).start()
        if k > 0:
            products(right, left)
        if k + 1 < planes:
            settle_b(k + 1)
        settle_a(k)
    settle_b(0)

    for k in range(planes):
        @pl.when(p != k)
        def _():
            grad_c_in(k).wait_recv()
    total = in_c[0].astype(F32)
    for k in range(1, planes):
        total += in_c[k].astype(F32)
    final[core, mine] = total.astype(BF16)
    for step in range(1, chips):
        grad_d(step).start()
    grad_e(0).start()
    for step in range(1, chips):
        grad_d(step).wait_recv()
        grad_e(step).start()
    for step in range(chips):
        grad_e(step).wait_recv()

    def square(i, carry):
        here = pl.ds(pl.multiple_of(i * CHUNK, CHUNK), CHUNK)
        for b in range(2):
            g = final[b, here].astype(F32)
            carry += g * g
        return carry

    squares = lax.fori_loop(0, n // CHUNK, square, jnp.zeros((CHUNK, h), F32))
    mean_square = jnp.sum(squares, keepdims=True) * (1.0 / (n * n))
    scale = 1.0 / jnp.sqrt(mean_square + EPSILON)

    def finish(i, carry):
        here = pl.ds(pl.multiple_of(i * CHUNK, CHUNK), CHUNK)
        for b in range(2):
            cols = slice(b * h, (b + 1) * h)
            out_ref[0, here, cols] = mask_ref[0, here, cols] + final[b, here].astype(F32) * scale
        return carry

    lax.fori_loop(0, n // CHUNK, finish, 0)

    for step in range(1, planes):
        mask_z(step).wait_send()
    for k in range(planes):
        @pl.when(p != k)
        def _():
            for step in range(1, chips):
                mask_layer(k, step).wait_send()
            mask_core(k).wait_send()
            grad_c(k).wait_send()

        grad_a(k).wait_send()
        for step in range(1, chips):
            grad_b(k, step).wait_send()
    for step in range(1, chips):
        grad_d(step).wait_send()
    for step in range(chips):
        grad_e(step).wait_send()


def shards(planes, modes, phase_masks, hg_orders, spot_index):
    n = phase_masks.shape[1]
    h = n // 2
    chips = modes // 2
    rows = n // chips
    others = max(chips - 1, 1)
    assert hg_orders.shape[0] == planes and n & (n - 1) == 0
    dma = pltpu.SemaphoreType.DMA
    vmem = pltpu.VMEM
    return pl.pallas_call(
        functools.partial(kernel, planes, modes),
        out_shape=jax.ShapeDtypeStruct((1, n, n), F32),
        in_specs=[
            pl.BlockSpec(memory_space=pltpu.SMEM),
            pl.BlockSpec(memory_space=pltpu.SMEM),
            pl.BlockSpec(memory_space=pltpu.VMEM),
        ],
        out_specs=pl.BlockSpec(memory_space=pltpu.VMEM),
        scratch_shapes=[
            vmem((planes, 2, n, h), BF16),
            vmem((planes, 2, n, h), F32),
            vmem((planes, 2, n, h), F32),
            vmem((planes, 2, n, h), BF16),
            vmem((planes, 2, n, h), BF16),
            vmem((2, n, n), BF16),
            vmem((2, n, n), BF16),
            vmem((2, n, n), F32),
            vmem((2, n, n), BF16),
            vmem((2, n, n), BF16),
            vmem((2, 2, h, h), F32),
            vmem((8, n), F32),
            vmem((n, 128), F32),
            vmem((planes, 2, n, h), BF16),
            vmem((planes, n, h), BF16),
            vmem((planes, n, h), BF16),
            vmem((planes, others, rows, h), BF16),
            vmem((planes, rows, h), BF16),
            vmem((planes, rows, h), BF16),
            vmem((2, n, h), BF16),
            dma((max(planes - 1, 1),)), dma((planes,)),
            dma((planes, others)), dma((planes, others)),
            dma((planes,)), dma((planes,)),
            dma((planes,)), dma((planes,)),
            dma((planes, others)), dma((planes, others)),
            dma((planes,)), dma((planes,)),
            dma((others,)), dma((others,)),
            dma((chips,)), dma((chips,)),
        ],
        compiler_params=pltpu.CompilerParams(
            collective_id=0, has_side_effects=True, vmem_limit_bytes=52 * 1024 * 1024
        ),
        name="phase_update",
    )(hg_orders.T, spot_index, phase_masks)


def solution(mesh):
    planes, modes = mesh.shape["plane"], mesh.shape["mode"]
    return jax.shard_map(
        functools.partial(shards, planes, modes),
        mesh=mesh,
        in_specs=(P("plane", None, None), P("mode", None), P("mode")),
        out_specs=P("plane", None, None),
        check_vma=False,
    )
```

```python
import functools
import math

import jax
import jax.numpy as jnp
from jax import lax
from jax.experimental import pallas as pl
from jax.experimental.pallas import tpu as pltpu
from jax.sharding import PartitionSpec as P

ORDERS = 45
SPOT_SIDE = 32
CHIRP_RATE = math.pi / 48.0 * (math.pi / 48.0)
AMPLITUDE = 12.0
EPSILON = 1e-06
CHUNK = 16
F32 = jnp.float32
BF16 = jnp.bfloat16
MESH = pl.DeviceIdType.MESH

SIN_HALF = [(-1.0) ** n / math.factorial(2 * n + 1) for n in range(6)]
COS_HALF = [(-1.0) ** n / math.factorial(2 * n) for n in range(6)]


def horner(u, coefficients):
    total = jnp.full_like(u, coefficients[-1])
    for value in coefficients[-2::-1]:
        total = total * u + value
    return total


def sincos(x):
    h = 0.5 * x
    u = h * h
    s = h * horner(u, SIN_HALF)
    c = horner(u, COS_HALF)
    return 2.0 * s * c, 1.0 - 2.0 * s * s


def quarter_tan(x):
    h = 0.5 * x
    u = h * h
    return h * horner(u, SIN_HALF) / (1.0 + horner(u, COS_HALF))


def sincos_of(t):
    twice = 2.0 / (1.0 + t * t)
    half_cos = twice - 1.0
    half_sin = t * twice
    double = 2.0 * half_sin
    return double * half_cos, 1.0 - double * half_sin


def split(x):
    high = x.astype(BF16)
    return high, (x - high.astype(F32)).astype(BF16)


def make_operators(n, left_ref, right_ref):
    h = n // 2
    rows = lax.broadcasted_iota(jnp.int32, (h, h), 0)
    slots = lax.broadcasted_iota(jnp.int32, (h, h), 1)
    for a in range(2):
        freq = 2 * slots + a
        turn = ((freq * rows + h) & (n - 1)) - h
        s, c = sincos(turn.astype(F32) * (2.0 * math.pi / n))
        basis = jnp.concatenate([c, s], axis=1)
        freq_row = 2 * lax.broadcasted_iota(jnp.int32, (8, h), 1) + a
        centred = ((freq_row + h) & (n - 1)) - h
        turns = (centred * centred).astype(F32) * (CHIRP_RATE / (2.0 * math.pi))
        turns = turns - jnp.floor(turns + 0.5)
        chirp_s, chirp_c = sincos(turns * (2.0 * math.pi))
        weighted = []
        for weight in (chirp_c, -chirp_s):
            weight = weight[:1] * (1.0 / n)
            weighted.append(basis * jnp.concatenate([weight, weight], axis=1))
        high, low = split(jnp.concatenate(weighted, axis=0))
        basis_high, basis_low = split(basis)
        prop = lax.dot_general(
            jnp.concatenate([high, high, low], axis=1),
            jnp.concatenate([basis_high, basis_low, basis_high], axis=1),
            (((1,), (1,)), ((), ())), preferred_element_type=F32,
        ).astype(BF16)
        re, im = prop[:h], prop[h:]
        left_ref[a, :h, :h] = re
        left_ref[a, :h, h:] = -im
        left_ref[a, h:, :h] = im
        left_ref[a, h:, h:] = re
        right_ref[a, :h, :h] = re
        right_ref[a, :h, h:] = im
        right_ref[a, h:, :h] = -im
        right_ref[a, h:, h:] = re


def make_tables(n, order_x, order_y, spot, right_ref, row_ref, col_ref):
    h = n // 2
    coords = lax.broadcasted_iota(jnp.int32, (8, n), 1).astype(F32) - (n - 1) / 2.0
    row_id = lax.broadcasted_iota(jnp.int32, (8, n), 0)
    orders = jnp.where(row_id == 0, order_x, order_y)
    scaled = coords * (48.0 / n)
    previous = math.pow(math.pi, -0.25) * jnp.exp(-0.5 * scaled * scaled)
    current = math.sqrt(2.0) * scaled * previous
    picked = jnp.where(orders == 0, previous, current)
    for degree in range(1, ORDERS - 1):
        higher = (
            math.sqrt(2.0 / (degree + 1.0)) * scaled * current
            - math.sqrt(degree / (degree + 1.0)) * previous
        )
        picked = jnp.where(orders == degree + 1, higher, picked)
        previous, current = current, higher
    centre = (SPOT_SIDE - 1) / 2.0
    spot_row = (spot // SPOT_SIDE).astype(F32) - centre
    spot_col = (spot % SPOT_SIDE).astype(F32) - centre
    place = jnp.where(row_id == 0, spot_row, spot_col)
    offset = (coords - (n / 40.0) * place) * (120.0 / n)
    profile = jnp.exp(-offset * offset)
    halves = []
    for a, folded in enumerate(
        (profile[:, :h] + profile[:, h:], profile[:, :h] - profile[:, h:])
    ):
        high, low = split(folded)
        both = jnp.dot(
            jnp.concatenate([high, low], axis=0), right_ref[a, :h], preferred_element_type=F32
        )
        halves.append(both[:8] + both[8:])
    spread = []
    for part in range(2):
        s, d = (half[:, part * h : (part + 1) * h] for half in halves)
        spread.append(jnp.concatenate([s + d, s - d], axis=1))
    table = jnp.concatenate(
        [
            AMPLITUDE * picked[0:1], picked[1:2],
            spread[0][0:1], spread[1][0:1], spread[0][1:2], spread[1][1:2],
            jnp.zeros((2, n), F32),
        ],
        axis=0,
    )
    row_ref[...] = table
    wide = jnp.concatenate([table, jnp.zeros((120, n), F32)], axis=0)
    col_ref[...] = wide.T


def kernel(
    planes, modes, orders_ref, spots_ref, mask_ref, out_ref,
    code, cosm, sinm, g_re, g_im, x_buf, w_buf, y_buf, left, right, row_tab, col_tab,
    grad, in_a, sum_a, in_b, piece, in_c, final,
    mz_s, mz_r, ml_s, ml_r, mc_s, mc_r, a_s, a_r, b_s, b_r, c_s, c_r, d_s, d_r, e_s, e_r,
):
    n = mask_ref.shape[-1]
    h = n // 2
    chips = modes // 2
    rows = n // chips
    p = lax.axis_index("plane")
    m = lax.axis_index("mode")
    core = m % 2
    chip = m // 2
    partner = m + 1 - 2 * core

    def at_chip(step):
        return (chip + step) % chips

    def rows_of(which):
        return pl.ds(pl.multiple_of(which * rows, rows), rows)

    def remote(src, dst, send, recv, plane=None, mode=None):
        return pltpu.make_async_remote_copy(
            src_ref=src, dst_ref=dst, send_sem=send, recv_sem=recv,
            device_id=(p if plane is None else plane, m if mode is None else mode),
            device_id_type=MESH,
        )

    mine = rows_of(chip)

    def mask_z(step):
        spot = code.at[p, core, mine]
        return remote(spot, spot, mz_s.at[step - 1], mz_r.at[p], plane=(p + step) % planes)

    def mask_z_in(k):
        spot = code.at[k, core, mine]
        return remote(spot, spot, mz_s.at[0], mz_r.at[k], plane=(p + 1) % planes)

    def mask_layer(k, step):
        spot = code.at[k, core, mine]
        return remote(
            spot, spot, ml_s.at[k, step - 1], ml_r.at[k, step - 1], mode=at_chip(step) * 2 + core
        )

    def mask_core(k):
        return remote(code.at[k, core], code.at[k, core], mc_s.at[k], mc_r.at[k], mode=partner)

    def grad_a(k):
        return remote(grad.at[k, 1 - core], in_a.at[k], a_s.at[k], a_r.at[k], mode=partner)

    def grad_b(k, step):
        there = at_chip(step)
        return remote(
            sum_a.at[k, rows_of(there)], in_b.at[k, step - 1], b_s.at[k, step - 1],
            b_r.at[k, step - 1], mode=there * 2 + core,
        )

    def grad_c(k):
        return remote(piece.at[k], in_c.at[p], c_s.at[k], c_r.at[p], plane=k)

    def grad_c_in(source):
        return remote(piece.at[0], in_c.at[source], c_s.at[0], c_r.at[source], plane=source)

    def grad_d(step):
        spot = final.at[core, mine]
        return remote(
            spot, spot, d_s.at[step - 1], d_r.at[step - 1], mode=at_chip(step) * 2 + core
        )

    def grad_e(step):
        spot = final.at[core, rows_of(at_chip(chips - step))]
        return remote(spot, spot, e_s.at[step], e_r.at[step], mode=partner)

    barrier = pltpu.get_barrier_semaphore()
    for step in range(1, planes):
        pl.semaphore_signal(
            barrier, inc=1, device_id=((p + step) % planes, m), device_id_type=MESH
        )
    for step in range(1, chips):
        pl.semaphore_signal(
            barrier, inc=1, device_id=(p, at_chip(step) * 2 + core), device_id_type=MESH
        )
    pl.semaphore_signal(barrier, inc=1, device_id=(p, partner), device_id_type=MESH)

    def encode(half, which):
        here = rows_of(which)
        cols = pl.ds(pl.multiple_of(half * h, h), h)
        code[p, half, here] = quarter_tan(mask_ref[0, here, cols]).astype(BF16)

    encode(core, chip)
    pl.semaphore_wait(barrier, planes - 1 + chips - 1 + 1)

    for step in range(1, planes):
        mask_z(step).start()

    encode(1 - core, chip)
    for step in range(1, chips):
        for half in range(2):
            encode(half, at_chip(step))
    make_operators(n, left, right)

    def spread_layer(k):
        @pl.when(p != k)
        def _():
            mask_z_in(k).wait_recv()
            for step in range(1, chips):
                mask_layer(k, step).start()

    def spread_core(k):
        @pl.when(p != k)
        def _():
            for step in range(1, chips):
                mask_layer(k, step).wait_recv()
            mask_core(k).start()

    for k in range(min(2, planes)):
        spread_layer(k)

    make_tables(
        n, orders_ref[0, p], orders_ref[1, p], spots_ref[p], right, row_tab, col_tab
    )
    spread_core(0)

    quads = [(a, b) for a in range(2) for b in range(2)]

    def span(i, a):
        return pl.ds(pl.multiple_of(a * h + i * CHUNK, CHUNK), CHUNK)

    def hadamard(q):
        top, bottom = q[0, 0] + q[0, 1], q[1, 0] + q[1, 1]
        top_d, bottom_d = q[0, 0] - q[0, 1], q[1, 0] - q[1, 1]
        return {
            (0, 0): top + bottom, (0, 1): top_d + bottom_d,
            (1, 0): top - bottom, (1, 1): top_d - bottom_d,
        }

    def combined(i):
        re = hadamard({(a, b): y_buf[b, span(i, a), :h] for a, b in quads})
        im = hadamard({(a, b): y_buf[b, span(i, a), h:] for a, b in quads})
        return re, im

    def put_sums(i, re, im):
        for part, q in enumerate((hadamard(re), hadamard(im))):
            for a, b in quads:
                x_buf[a, span(i, part), b * h : (b + 1) * h] = q[a, b].astype(BF16)

    def products(first, second):
        for a in range(2):
            v = jnp.dot(first[a], x_buf[a], preferred_element_type=F32)
            for b in range(2):
                for part in range(2):
                    w_buf[b, a * h : (a + 1) * h, part * h : (part + 1) * h] = v[
                        part * h : (part + 1) * h, b * h : (b + 1) * h
                    ].astype(BF16)
        for b in range(2):
            y_buf[b] = jnp.dot(w_buf[b], second[b], preferred_element_type=F32)

    def outer(i, a, b):
        ar, ai = col_tab[span(i, a), 2:3], col_tab[span(i, a), 3:4]
        br, bi = row_tab[4:5, b * h : (b + 1) * h], row_tab[5:6, b * h : (b + 1) * h]
        return ar * br - ai * bi, ar * bi + ai * br

    for k in range(planes):
        @pl.when(p != k)
        def _():
            mask_core(k).wait_recv()

        if k + 2 < planes:
            spread_layer(k + 2)
        last = k == planes - 1

        def forward(i, carry):
            if k == 0:
                field_re = {
                    (a, b): col_tab[span(i, a), 0:1] * row_tab[1:2, b * h : (b + 1) * h]
                    for a, b in quads
                }
                field_im = None
            else:
                field_re, field_im = combined(i)
            masked_re, masked_im = {}, {}
            for a, b in quads:
                s, c = sincos_of(code[k, b, span(i, a)].astype(F32))
                cosm[k, b, span(i, a)] = c
                sinm[k, b, span(i, a)] = s
                if field_im is None:
                    re, im = field_re[a, b] * c, field_re[a, b] * s
                else:
                    fr, fi = field_re[a, b], field_im[a, b]
                    re, im = fr * c - fi * s, fr * s + fi * c
                masked_re[a, b], masked_im[a, b] = re, im
                g_re[k, b, span(i, a)] = re.astype(BF16)
                g_im[k, b, span(i, a)] = im.astype(BF16)
            if not last:
                put_sums(i, masked_re, masked_im)
                return carry
            total_re, total_im = carry
            for a, b in quads:
                er, ei = outer(i, a, b)
                re, im = masked_re[a, b], masked_im[a, b]
                total_re += er * re - ei * im
                total_im += er * im + ei * re
            return total_re, total_im

        zero = jnp.zeros((CHUNK, h), F32)
        totals = lax.fori_loop(0, h // CHUNK, forward, (zero, zero) if last else 0)
        if not last:
            spread_core(k + 1)
            products(left, right)
    coupling_re = jnp.sum(totals[0], keepdims=True)
    coupling_im = jnp.sum(totals[1], keepdims=True)

    def settle_a(k):
        grad_a(k).wait_recv()
        sum_a[k] = (grad[k, core].astype(F32) + in_a[k].astype(F32)).astype(BF16)
        for step in range(1, chips):
            grad_b(k, step).start()

    def settle_b(k):
        for step in range(1, chips):
            grad_b(k, step).wait_recv()
        total = sum_a[k, mine].astype(F32)
        for step in range(1, chips):
            total += in_b[k, step - 1].astype(F32)
        piece[k] = total.astype(BF16)

        @pl.when(p != k)
        def _():
            grad_c(k).start()

        @pl.when(p == k)
        def _():
            in_c[k] = piece[k]

    for k in range(planes - 1, -1, -1):
        def backward(i, carry):
            if k == planes - 1:
                back_re, back_im = {}, {}
                for a, b in quads:
                    er, ei = outer(i, a, b)
                    back_re[a, b] = coupling_re * er + coupling_im * ei
                    back_im[a, b] = coupling_im * er - coupling_re * ei
            else:
                back_re, back_im = combined(i)
            reply_re, reply_im = {}, {}
            for a, b in quads:
                br, bi = back_re[a, b], back_im[a, b]
                gr = g_re[k, b, span(i, a)].astype(F32)
                gi = g_im[k, b, span(i, a)].astype(F32)
                grad[k, b, span(i, a)] = (2.0 * (bi * gr - br * gi)).astype(BF16)
                if k > 0:
                    c, s = cosm[k, b, span(i, a)], sinm[k, b, span(i, a)]
                    reply_re[a, b] = br * c + bi * s
                    reply_im[a, b] = bi * c - br * s
            if k > 0:
                put_sums(i, reply_re, reply_im)
            return carry

        lax.fori_loop(0, h // CHUNK, backward, 0)
        grad_a(k).start()
        if k > 0:
            products(right, left)
        if k + 1 < planes:
            settle_b(k + 1)
        settle_a(k)
    settle_b(0)

    for k in range(planes):
        @pl.when(p != k)
        def _():
            grad_c_in(k).wait_recv()
    total = in_c[0].astype(F32)
    for k in range(1, planes):
        total += in_c[k].astype(F32)
    final[core, mine] = total.astype(BF16)
    for step in range(1, chips):
        grad_d(step).start()
    grad_e(0).start()
    for step in range(1, chips):
        grad_d(step).wait_recv()
        grad_e(step).start()
    for step in range(chips):
        grad_e(step).wait_recv()

    def square(i, carry):
        here = pl.ds(pl.multiple_of(i * CHUNK, CHUNK), CHUNK)
        for b in range(2):
            g = final[b, here].astype(F32)
            carry += g * g
        return carry

    squares = lax.fori_loop(0, n // CHUNK, square, jnp.zeros((CHUNK, h), F32))
    mean_square = jnp.sum(squares, keepdims=True) * (1.0 / (n * n))
    scale = 1.0 / jnp.sqrt(mean_square + EPSILON)

    def finish(i, carry):
        here = pl.ds(pl.multiple_of(i * CHUNK, CHUNK), CHUNK)
        for b in range(2):
            cols = slice(b * h, (b + 1) * h)
            out_ref[0, here, cols] = mask_ref[0, here, cols] + final[b, here].astype(F32) * scale
        return carry

    lax.fori_loop(0, n // CHUNK, finish, 0)

    for step in range(1, planes):
        mask_z(step).wait_send()
    for k in range(planes):
        @pl.when(p != k)
        def _():
            for step in range(1, chips):
                mask_layer(k, step).wait_send()
            mask_core(k).wait_send()
            grad_c(k).wait_send()

        grad_a(k).wait_send()
        for step in range(1, chips):
            grad_b(k, step).wait_send()
    for step in range(1, chips):
        grad_d(step).wait_send()
    for step in range(chips):
        grad_e(step).wait_send()


def shards(planes, modes, phase_masks, hg_orders, spot_index):
    n = phase_masks.shape[1]
    h = n // 2
    chips = modes // 2
    rows = n // chips
    others = max(chips - 1, 1)
    assert hg_orders.shape[0] == planes and n & (n - 1) == 0
    dma = pltpu.SemaphoreType.DMA
    vmem = pltpu.VMEM
    return pl.pallas_call(
        functools.partial(kernel, planes, modes),
        out_shape=jax.ShapeDtypeStruct((1, n, n), F32),
        in_specs=[
            pl.BlockSpec(memory_space=pltpu.SMEM),
            pl.BlockSpec(memory_space=pltpu.SMEM),
            pl.BlockSpec(memory_space=pltpu.VMEM),
        ],
        out_specs=pl.BlockSpec(memory_space=pltpu.VMEM),
        scratch_shapes=[
            vmem((planes, 2, n, h), BF16),
            vmem((planes, 2, n, h), F32),
            vmem((planes, 2, n, h), F32),
            vmem((planes, 2, n, h), BF16),
            vmem((planes, 2, n, h), BF16),
            vmem((2, n, n), BF16),
            vmem((2, n, n), BF16),
            vmem((2, n, n), F32),
            vmem((2, n, n), BF16),
            vmem((2, n, n), BF16),
            vmem((8, n), F32),
            vmem((n, 128), F32),
            vmem((planes, 2, n, h), BF16),
            vmem((planes, n, h), BF16),
            vmem((planes, n, h), BF16),
            vmem((planes, others, rows, h), BF16),
            vmem((planes, rows, h), BF16),
            vmem((planes, rows, h), BF16),
            vmem((2, n, h), BF16),
            dma((max(planes - 1, 1),)), dma((planes,)),
            dma((planes, others)), dma((planes, others)),
            dma((planes,)), dma((planes,)),
            dma((planes,)), dma((planes,)),
            dma((planes, others)), dma((planes, others)),
            dma((planes,)), dma((planes,)),
            dma((others,)), dma((others,)),
            dma((chips,)), dma((chips,)),
        ],
        compiler_params=pltpu.CompilerParams(
            collective_id=0, has_side_effects=True, vmem_limit_bytes=52 * 1024 * 1024
        ),
        name="phase_update",
    )(hg_orders.T, spot_index, phase_masks)


def solution(mesh):
    planes, modes = mesh.shape["plane"], mesh.shape["mode"]
    return jax.shard_map(
        functools.partial(shards, planes, modes),
        mesh=mesh,
        in_specs=(P("plane", None, None), P("mode", None), P("mode")),
        out_specs=P("plane", None, None),
        check_vma=False,
    )
```

```python
import functools
import math

import jax
import jax.numpy as jnp
from jax import lax
from jax.experimental import pallas as pl
from jax.experimental.pallas import tpu as pltpu
from jax.sharding import PartitionSpec as P

ORDERS = 45
SPOT_SIDE = 32
CHIRP_RATE = math.pi / 48.0 * (math.pi / 48.0)
AMPLITUDE = 12.0
EPSILON = 1e-06
CHUNK = 16
STRIP = 128
F32 = jnp.float32
BF16 = jnp.bfloat16
MESH = pl.DeviceIdType.MESH

SIN_HALF = [(-1.0) ** n / math.factorial(2 * n + 1) for n in range(6)]
COS_HALF = [(-1.0) ** n / math.factorial(2 * n) for n in range(6)]


def horner(u, coefficients):
    total = jnp.full_like(u, coefficients[-1])
    for value in coefficients[-2::-1]:
        total = total * u + value
    return total


def sincos(x):
    h = 0.5 * x
    u = h * h
    s = h * horner(u, SIN_HALF)
    c = horner(u, COS_HALF)
    return 2.0 * s * c, 1.0 - 2.0 * s * s


def quarter_tan(x):
    h = 0.5 * x
    u = h * h
    return h * horner(u, SIN_HALF) / (1.0 + horner(u, COS_HALF))


def sincos_of(t):
    twice = 2.0 / (1.0 + t * t)
    half_cos = twice - 1.0
    half_sin = t * twice
    double = 2.0 * half_sin
    return double * half_cos, 1.0 - double * half_sin


def split(x):
    high = x.astype(BF16)
    return high, (x - high.astype(F32)).astype(BF16)


def make_operators(n, left_ref, right_ref):
    h = n // 2
    rows = lax.broadcasted_iota(jnp.int32, (h, h), 0)
    slots = lax.broadcasted_iota(jnp.int32, (h, h), 1)
    for a in range(2):
        freq = 2 * slots + a
        turn = ((freq * rows + h) & (n - 1)) - h
        s, c = sincos(turn.astype(F32) * (2.0 * math.pi / n))
        basis = jnp.concatenate([c, s], axis=1)
        freq_row = 2 * lax.broadcasted_iota(jnp.int32, (8, h), 1) + a
        centred = ((freq_row + h) & (n - 1)) - h
        turns = (centred * centred).astype(F32) * (CHIRP_RATE / (2.0 * math.pi))
        turns = turns - jnp.floor(turns + 0.5)
        chirp_s, chirp_c = sincos(turns * (2.0 * math.pi))
        weighted = []
        for weight in (chirp_c, -chirp_s):
            weight = weight[:1] * (1.0 / n)
            weighted.append(basis * jnp.concatenate([weight, weight], axis=1))
        high, low = split(jnp.concatenate(weighted, axis=0))
        basis_high, basis_low = split(basis)
        prop = lax.dot_general(
            jnp.concatenate([high, high, low], axis=1),
            jnp.concatenate([basis_high, basis_low, basis_high], axis=1),
            (((1,), (1,)), ((), ())), preferred_element_type=F32,
        ).astype(BF16)
        re, im = prop[:h], prop[h:]
        left_ref[a, :h, :h] = re
        left_ref[a, :h, h:] = -im
        left_ref[a, h:, :h] = im
        left_ref[a, h:, h:] = re
        right_ref[a, :h, :h] = re
        right_ref[a, :h, h:] = im
        right_ref[a, h:, :h] = -im
        right_ref[a, h:, h:] = re


def make_tables(n, order_x, order_y, spot, right_ref, row_ref, col_ref):
    h = n // 2
    coords = lax.broadcasted_iota(jnp.int32, (8, n), 1).astype(F32) - (n - 1) / 2.0
    row_id = lax.broadcasted_iota(jnp.int32, (8, n), 0)
    orders = jnp.where(row_id == 0, order_x, order_y)
    scaled = coords * (48.0 / n)
    previous = math.pow(math.pi, -0.25) * jnp.exp(-0.5 * scaled * scaled)
    current = math.sqrt(2.0) * scaled * previous
    picked = jnp.where(orders == 0, previous, current)
    for degree in range(1, ORDERS - 1):
        higher = (
            math.sqrt(2.0 / (degree + 1.0)) * scaled * current
            - math.sqrt(degree / (degree + 1.0)) * previous
        )
        picked = jnp.where(orders == degree + 1, higher, picked)
        previous, current = current, higher
    centre = (SPOT_SIDE - 1) / 2.0
    spot_row = (spot // SPOT_SIDE).astype(F32) - centre
    spot_col = (spot % SPOT_SIDE).astype(F32) - centre
    place = jnp.where(row_id == 0, spot_row, spot_col)
    offset = (coords - (n / 40.0) * place) * (120.0 / n)
    profile = jnp.exp(-offset * offset)
    halves = []
    for a, folded in enumerate(
        (profile[:, :h] + profile[:, h:], profile[:, :h] - profile[:, h:])
    ):
        high, low = split(folded)
        both = jnp.dot(
            jnp.concatenate([high, low], axis=0), right_ref[a, :h], preferred_element_type=F32
        )
        halves.append(both[:8] + both[8:])
    spread = []
    for part in range(2):
        s, d = (half[:, part * h : (part + 1) * h] for half in halves)
        spread.append(jnp.concatenate([s + d, s - d], axis=1))
    table = jnp.concatenate(
        [
            AMPLITUDE * picked[0:1], picked[1:2],
            spread[0][0:1], spread[1][0:1], spread[0][1:2], spread[1][1:2],
            jnp.zeros((2, n), F32),
        ],
        axis=0,
    )
    row_ref[...] = table
    wide = jnp.concatenate([table, jnp.zeros((120, n), F32)], axis=0)
    col_ref[...] = wide.T


def kernel(
    planes, modes, orders_ref, spots_ref, mask_ref, out_ref,
    code, cosm, sinm, g_re, g_im, x_buf, w_buf, y_buf, left, right, row_tab, col_tab,
    grad, in_a, sum_a, in_b, piece, in_c, final,
    mz_s, mz_r, ml_s, ml_r, mc_s, mc_r, a_s, a_r, b_s, b_r, c_s, c_r, d_s, d_r, e_s, e_r,
):
    n = mask_ref.shape[-1]
    h = n // 2
    chips = modes // 2
    rows = n // chips
    p = lax.axis_index("plane")
    m = lax.axis_index("mode")
    core = m % 2
    chip = m // 2
    partner = m + 1 - 2 * core

    def at_chip(step):
        return (chip + step) % chips

    def rows_of(which):
        return pl.ds(pl.multiple_of(which * rows, rows), rows)

    def remote(src, dst, send, recv, plane=None, mode=None):
        return pltpu.make_async_remote_copy(
            src_ref=src, dst_ref=dst, send_sem=send, recv_sem=recv,
            device_id=(p if plane is None else plane, m if mode is None else mode),
            device_id_type=MESH,
        )

    mine = rows_of(chip)

    def mask_z(step):
        spot = code.at[p, core, mine]
        return remote(spot, spot, mz_s.at[step - 1], mz_r.at[p], plane=(p + step) % planes)

    def mask_z_in(k):
        spot = code.at[k, core, mine]
        return remote(spot, spot, mz_s.at[0], mz_r.at[k], plane=(p + 1) % planes)

    def mask_layer(k, step):
        spot = code.at[k, core, mine]
        return remote(
            spot, spot, ml_s.at[k, step - 1], ml_r.at[k, step - 1], mode=at_chip(step) * 2 + core
        )

    def mask_core(k):
        return remote(code.at[k, core], code.at[k, core], mc_s.at[k], mc_r.at[k], mode=partner)

    parts = in_b.shape[2]
    size = rows // parts

    def part_rows(which, q):
        return pl.ds(pl.multiple_of(q * (n // parts) + which * size, size), size)

    def half_rows(q):
        return pl.ds(q * (n // parts), n // parts)

    def grad_a(k, q):
        return remote(
            grad.at[k, 1 - core, half_rows(q)], in_a.at[k, half_rows(q)],
            a_s.at[k, q], a_r.at[k, q], mode=partner,
        )

    def grad_b(k, q, step):
        there = at_chip(step)
        return remote(
            sum_a.at[k, part_rows(there, q)], in_b.at[k, step - 1, q], b_s.at[k, q, step - 1],
            b_r.at[k, q, step - 1], mode=there * 2 + core,
        )

    def grad_c(k, q):
        return remote(piece.at[k, q], in_c.at[p, q], c_s.at[k, q], c_r.at[p, q], plane=k)

    def grad_c_in(source, q):
        return remote(
            piece.at[0, q], in_c.at[source, q], c_s.at[0, q], c_r.at[source, q], plane=source
        )

    def grad_d(q, step):
        spot = final.at[core, part_rows(chip, q)]
        return remote(
            spot, spot, d_s.at[q, step - 1], d_r.at[q, step - 1], mode=at_chip(step) * 2 + core
        )

    def grad_e(q, step):
        spot = final.at[core, part_rows(at_chip(chips - step), q)]
        return remote(spot, spot, e_s.at[q, step], e_r.at[q, step], mode=partner)

    barrier = pltpu.get_barrier_semaphore()
    for step in range(1, planes):
        pl.semaphore_signal(
            barrier, inc=1, device_id=((p + step) % planes, m), device_id_type=MESH
        )
    for step in range(1, chips):
        pl.semaphore_signal(
            barrier, inc=1, device_id=(p, at_chip(step) * 2 + core), device_id_type=MESH
        )
    pl.semaphore_signal(barrier, inc=1, device_id=(p, partner), device_id_type=MESH)

    def encode(half, which):
        here = rows_of(which)
        cols = pl.ds(pl.multiple_of(half * h, h), h)
        code[p, half, here] = quarter_tan(mask_ref[0, here, cols]).astype(BF16)

    encode(core, chip)
    pl.semaphore_wait(barrier, planes - 1 + chips - 1 + 1)

    for step in range(1, planes):
        mask_z(step).start()

    encode(1 - core, chip)
    for step in range(1, chips):
        for half in range(2):
            encode(half, at_chip(step))
    make_operators(n, left, right)

    def spread_layer(k):
        @pl.when(p != k)
        def _():
            mask_z_in(k).wait_recv()
            for step in range(1, chips):
                mask_layer(k, step).start()

    def spread_core(k):
        @pl.when(p != k)
        def _():
            for step in range(1, chips):
                mask_layer(k, step).wait_recv()
            mask_core(k).start()

    for k in range(min(2, planes)):
        spread_layer(k)

    make_tables(
        n, orders_ref[0, p], orders_ref[1, p], spots_ref[p], right, row_tab, col_tab
    )
    spread_core(0)

    quads = [(a, b) for a in range(2) for b in range(2)]

    def span(i, a):
        return pl.ds(pl.multiple_of(a * h + i * CHUNK, CHUNK), CHUNK)

    def hadamard(q):
        top, bottom = q[0, 0] + q[0, 1], q[1, 0] + q[1, 1]
        top_d, bottom_d = q[0, 0] - q[0, 1], q[1, 0] - q[1, 1]
        return {
            (0, 0): top + bottom, (0, 1): top_d + bottom_d,
            (1, 0): top - bottom, (1, 1): top_d - bottom_d,
        }

    strips = [slice(at, at + STRIP) for at in range(0, h, STRIP)]

    def columns(strip, b):
        return slice(b * h + strip.start, b * h + strip.stop)

    def combined(i, strip):
        re = hadamard({(a, b): y_buf[b, span(i, a), columns(strip, 0)] for a, b in quads})
        im = hadamard({(a, b): y_buf[b, span(i, a), columns(strip, 1)] for a, b in quads})
        return re, im

    def put_sums(i, strip, re, im):
        for part, q in enumerate((hadamard(re), hadamard(im))):
            for a, b in quads:
                x_buf[a, span(i, part), columns(strip, b)] = q[a, b].astype(BF16)

    def products(first, second):
        for a in range(2):
            v = jnp.dot(first[a], x_buf[a], preferred_element_type=F32)
            for b in range(2):
                for part in range(2):
                    w_buf[b, a * h : (a + 1) * h, part * h : (part + 1) * h] = v[
                        part * h : (part + 1) * h, b * h : (b + 1) * h
                    ].astype(BF16)
        for b in range(2):
            y_buf[b] = jnp.dot(w_buf[b], second[b], preferred_element_type=F32)

    def outer(i, strip, a, b):
        ar, ai = col_tab[span(i, a), 2:3], col_tab[span(i, a), 3:4]
        br, bi = row_tab[4:5, columns(strip, b)], row_tab[5:6, columns(strip, b)]
        return ar * br - ai * bi, ar * bi + ai * br

    for k in range(planes):
        @pl.when(p != k)
        def _():
            mask_core(k).wait_recv()

        if k + 2 < planes:
            spread_layer(k + 2)
        last = k == planes - 1

        def forward(i, carry):
            for strip in strips:
                carry = forward_strip(i, strip, carry)
            return carry

        def forward_strip(i, strip, carry):
            if k == 0:
                field_re = {
                    (a, b): col_tab[span(i, a), 0:1] * row_tab[1:2, columns(strip, b)]
                    for a, b in quads
                }
                field_im = None
            else:
                field_re, field_im = combined(i, strip)
            masked_re, masked_im = {}, {}
            for a, b in quads:
                s, c = sincos_of(code[k, b, span(i, a), strip].astype(F32))
                cosm[k, b, span(i, a), strip] = c
                sinm[k, b, span(i, a), strip] = s
                if field_im is None:
                    re, im = field_re[a, b] * c, field_re[a, b] * s
                else:
                    fr, fi = field_re[a, b], field_im[a, b]
                    re, im = fr * c - fi * s, fr * s + fi * c
                masked_re[a, b], masked_im[a, b] = re, im
                g_re[k, b, span(i, a), strip] = re.astype(BF16)
                g_im[k, b, span(i, a), strip] = im.astype(BF16)
            if not last:
                put_sums(i, strip, masked_re, masked_im)
                return carry
            total_re, total_im = carry
            for a, b in quads:
                er, ei = outer(i, strip, a, b)
                re, im = masked_re[a, b], masked_im[a, b]
                total_re += er * re - ei * im
                total_im += er * im + ei * re
            return total_re, total_im

        zero = jnp.zeros((CHUNK, STRIP), F32)
        totals = lax.fori_loop(0, h // CHUNK, forward, (zero, zero) if last else 0)
        if not last:
            spread_core(k + 1)
            products(left, right)
    coupling_re = jnp.sum(totals[0], keepdims=True)
    coupling_im = jnp.sum(totals[1], keepdims=True)

    def settle_a(k, q):
        grad_a(k, q).wait_recv()
        here = half_rows(q)
        sum_a[k, here] = (grad[k, core, here].astype(F32) + in_a[k, here].astype(F32)).astype(BF16)
        for step in range(1, chips):
            grad_b(k, q, step).start()

    def settle_b(k, q):
        for step in range(1, chips):
            grad_b(k, q, step).wait_recv()
        total = sum_a[k, part_rows(chip, q)].astype(F32)
        for step in range(1, chips):
            total += in_b[k, step - 1, q].astype(F32)
        piece[k, q] = total.astype(BF16)

        @pl.when(p != k)
        def _():
            grad_c(k, q).start()

        @pl.when(p == k)
        def _():
            in_c[k, q] = piece[k, q]

    for k in range(planes - 1, -1, -1):
        def backward(i, carry):
            for strip in strips:
                backward_strip(i, strip)
            return carry

        def backward_strip(i, strip):
            if k == planes - 1:
                back_re, back_im = {}, {}
                for a, b in quads:
                    er, ei = outer(i, strip, a, b)
                    back_re[a, b] = coupling_re * er + coupling_im * ei
                    back_im[a, b] = coupling_im * er - coupling_re * ei
            else:
                back_re, back_im = combined(i, strip)
            reply_re, reply_im = {}, {}
            for a, b in quads:
                br, bi = back_re[a, b], back_im[a, b]
                gr = g_re[k, b, span(i, a), strip].astype(F32)
                gi = g_im[k, b, span(i, a), strip].astype(F32)
                grad[k, b, span(i, a), strip] = (2.0 * (bi * gr - br * gi)).astype(BF16)
                if k > 0:
                    c, s = cosm[k, b, span(i, a), strip], sinm[k, b, span(i, a), strip]
                    reply_re[a, b] = br * c + bi * s
                    reply_im[a, b] = bi * c - br * s
            if k > 0:
                put_sums(i, strip, reply_re, reply_im)

        lax.fori_loop(0, h // CHUNK, backward, 0)
        for q in range(parts):
            grad_a(k, q).start()
        if k > 0:
            products(right, left)
        for q in range(parts):
            if k + 1 < planes:
                settle_b(k + 1, q)
        for q in range(parts):
            settle_a(k, q)
    for q in range(parts):
        settle_b(0, q)

    for q in range(parts):
        for k in range(planes):
            @pl.when(p != k)
            def _():
                grad_c_in(k, q).wait_recv()
        total = in_c[0, q].astype(F32)
        for k in range(1, planes):
            total += in_c[k, q].astype(F32)
        final[core, part_rows(chip, q)] = total.astype(BF16)
        for step in range(1, chips):
            grad_d(q, step).start()
        grad_e(q, 0).start()
    for q in range(parts):
        for step in range(1, chips):
            grad_d(q, step).wait_recv()
            grad_e(q, step).start()
    for q in range(parts):
        for step in range(chips):
            grad_e(q, step).wait_recv()

    def square(i, carry):
        here = pl.ds(pl.multiple_of(i * CHUNK, CHUNK), CHUNK)
        for b in range(2):
            g = final[b, here].astype(F32)
            carry += g * g
        return carry

    squares = lax.fori_loop(0, n // CHUNK, square, jnp.zeros((CHUNK, h), F32))
    mean_square = jnp.sum(squares, keepdims=True) * (1.0 / (n * n))
    scale = 1.0 / jnp.sqrt(mean_square + EPSILON)

    def finish(i, carry):
        here = pl.ds(pl.multiple_of(i * CHUNK, CHUNK), CHUNK)
        for b in range(2):
            cols = slice(b * h, (b + 1) * h)
            out_ref[0, here, cols] = mask_ref[0, here, cols] + final[b, here].astype(F32) * scale
        return carry

    lax.fori_loop(0, n // CHUNK, finish, 0)

    for step in range(1, planes):
        mask_z(step).wait_send()
    for k in range(planes):
        @pl.when(p != k)
        def _():
            for step in range(1, chips):
                mask_layer(k, step).wait_send()
            mask_core(k).wait_send()
            for q in range(parts):
                grad_c(k, q).wait_send()

        for q in range(parts):
            grad_a(k, q).wait_send()
            for step in range(1, chips):
                grad_b(k, q, step).wait_send()
    for q in range(parts):
        for step in range(1, chips):
            grad_d(q, step).wait_send()
        for step in range(chips):
            grad_e(q, step).wait_send()


def shards(planes, modes, phase_masks, hg_orders, spot_index):
    n = phase_masks.shape[1]
    h = n // 2
    chips = modes // 2
    rows = n // chips
    others = max(chips - 1, 1)
    parts = 2 if rows % 32 == 0 else 1
    assert hg_orders.shape[0] == planes and n & (n - 1) == 0
    dma = pltpu.SemaphoreType.DMA
    vmem = pltpu.VMEM
    return pl.pallas_call(
        functools.partial(kernel, planes, modes),
        out_shape=jax.ShapeDtypeStruct((1, n, n), F32),
        in_specs=[
            pl.BlockSpec(memory_space=pltpu.SMEM),
            pl.BlockSpec(memory_space=pltpu.SMEM),
            pl.BlockSpec(memory_space=pltpu.VMEM),
        ],
        out_specs=pl.BlockSpec(memory_space=pltpu.VMEM),
        scratch_shapes=[
            vmem((planes, 2, n, h), BF16),
            vmem((planes, 2, n, h), F32),
            vmem((planes, 2, n, h), F32),
            vmem((planes, 2, n, h), BF16),
            vmem((planes, 2, n, h), BF16),
            vmem((2, n, n), BF16),
            vmem((2, n, n), BF16),
            vmem((2, n, n), F32),
            vmem((2, n, n), BF16),
            vmem((2, n, n), BF16),
            vmem((8, n), F32),
            vmem((n, 128), F32),
            vmem((planes, 2, n, h), BF16),
            vmem((planes, n, h), BF16),
            vmem((planes, n, h), BF16),
            vmem((planes, others, parts, rows // parts, h), BF16),
            vmem((planes, parts, rows // parts, h), BF16),
            vmem((planes, parts, rows // parts, h), BF16),
            vmem((2, n, h), BF16),
            dma((max(planes - 1, 1),)), dma((planes,)),
            dma((planes, others)), dma((planes, others)),
            dma((planes,)), dma((planes,)),
            dma((planes, parts)), dma((planes, parts)),
            dma((planes, parts, others)), dma((planes, parts, others)),
            dma((planes, parts)), dma((planes, parts)),
            dma((parts, others)), dma((parts, others)),
            dma((parts, chips)), dma((parts, chips)),
        ],
        compiler_params=pltpu.CompilerParams(
            collective_id=0, has_side_effects=True, vmem_limit_bytes=52 * 1024 * 1024
        ),
        name="phase_update",
    )(hg_orders.T, spot_index, phase_masks)


def solution(mesh):
    planes, modes = mesh.shape["plane"], mesh.shape["mode"]
    return jax.shard_map(
        functools.partial(shards, planes, modes),
        mesh=mesh,
        in_specs=(P("plane", None, None), P("mode", None), P("mode")),
        out_specs=P("plane", None, None),
        check_vma=False,
    )
```

```python
import functools
import math

import jax
import jax.numpy as jnp
from jax import lax
from jax.experimental import pallas as pl
from jax.experimental.pallas import tpu as pltpu
from jax.sharding import PartitionSpec as P

ORDERS = 45
SPOT_SIDE = 32
CHIRP_RATE = math.pi / 48.0 * (math.pi / 48.0)
AMPLITUDE = 12.0
EPSILON = 1e-06
CHUNK = 16
STRIP = 128
F32 = jnp.float32
BF16 = jnp.bfloat16
MESH = pl.DeviceIdType.MESH

SIN_HALF = [(-1.0) ** n / math.factorial(2 * n + 1) for n in range(6)]
COS_HALF = [(-1.0) ** n / math.factorial(2 * n) for n in range(6)]


def horner(u, coefficients):
    total = jnp.full_like(u, coefficients[-1])
    for value in coefficients[-2::-1]:
        total = total * u + value
    return total


def sincos(x):
    h = 0.5 * x
    u = h * h
    s = h * horner(u, SIN_HALF)
    c = horner(u, COS_HALF)
    return 2.0 * s * c, 1.0 - 2.0 * s * s


def quarter_tan(x):
    h = 0.5 * x
    u = h * h
    return h * horner(u, SIN_HALF) / (1.0 + horner(u, COS_HALF))


def sincos_of(t):
    twice = 2.0 / (1.0 + t * t)
    half_cos = twice - 1.0
    half_sin = t * twice
    double = 2.0 * half_sin
    return double * half_cos, 1.0 - double * half_sin


def split(x):
    high = x.astype(BF16)
    return high, (x - high.astype(F32)).astype(BF16)


def make_operators(n, left_ref, right_ref):
    h = n // 2
    rows = lax.broadcasted_iota(jnp.int32, (h, h), 0)
    slots = lax.broadcasted_iota(jnp.int32, (h, h), 1)
    for a in range(2):
        freq = 2 * slots + a
        turn = ((freq * rows + h) & (n - 1)) - h
        s, c = sincos(turn.astype(F32) * (2.0 * math.pi / n))
        basis = jnp.concatenate([c, s], axis=1)
        freq_row = 2 * lax.broadcasted_iota(jnp.int32, (8, h), 1) + a
        centred = ((freq_row + h) & (n - 1)) - h
        turns = (centred * centred).astype(F32) * (CHIRP_RATE / (2.0 * math.pi))
        turns = turns - jnp.floor(turns + 0.5)
        chirp_s, chirp_c = sincos(turns * (2.0 * math.pi))
        weighted = []
        for weight in (chirp_c, -chirp_s):
            weight = weight[:1] * (1.0 / n)
            weighted.append(basis * jnp.concatenate([weight, weight], axis=1))
        high, low = split(jnp.concatenate(weighted, axis=0))
        basis_high, basis_low = split(basis)
        prop = lax.dot_general(
            jnp.concatenate([high, high, low], axis=1),
            jnp.concatenate([basis_high, basis_low, basis_high], axis=1),
            (((1,), (1,)), ((), ())), preferred_element_type=F32,
        ).astype(BF16)
        re, im = prop[:h], prop[h:]
        left_ref[a, :h, :h] = re
        left_ref[a, :h, h:] = -im
        left_ref[a, h:, :h] = im
        left_ref[a, h:, h:] = re
        right_ref[a, :h, :h] = re
        right_ref[a, :h, h:] = im
        right_ref[a, h:, :h] = -im
        right_ref[a, h:, h:] = re


def make_tables(n, order_x, order_y, spot, right_ref, row_ref, col_ref):
    h = n // 2
    coords = lax.broadcasted_iota(jnp.int32, (8, n), 1).astype(F32) - (n - 1) / 2.0
    row_id = lax.broadcasted_iota(jnp.int32, (8, n), 0)
    orders = jnp.where(row_id == 0, order_x, order_y)
    scaled = coords * (48.0 / n)
    previous = math.pow(math.pi, -0.25) * jnp.exp(-0.5 * scaled * scaled)
    current = math.sqrt(2.0) * scaled * previous
    picked = jnp.where(orders == 0, previous, current)
    for degree in range(1, ORDERS - 1):
        higher = (
            math.sqrt(2.0 / (degree + 1.0)) * scaled * current
            - math.sqrt(degree / (degree + 1.0)) * previous
        )
        picked = jnp.where(orders == degree + 1, higher, picked)
        previous, current = current, higher
    centre = (SPOT_SIDE - 1) / 2.0
    spot_row = (spot // SPOT_SIDE).astype(F32) - centre
    spot_col = (spot % SPOT_SIDE).astype(F32) - centre
    place = jnp.where(row_id == 0, spot_row, spot_col)
    offset = (coords - (n / 40.0) * place) * (120.0 / n)
    profile = jnp.exp(-offset * offset)
    halves = []
    for a, folded in enumerate(
        (profile[:, :h] + profile[:, h:], profile[:, :h] - profile[:, h:])
    ):
        high, low = split(folded)
        both = jnp.dot(
            jnp.concatenate([high, low], axis=0), right_ref[a, :h], preferred_element_type=F32
        )
        halves.append(both[:8] + both[8:])
    spread = []
    for part in range(2):
        s, d = (half[:, part * h : (part + 1) * h] for half in halves)
        spread.append(jnp.concatenate([s + d, s - d], axis=1))
    table = jnp.concatenate(
        [
            AMPLITUDE * picked[0:1], picked[1:2],
            spread[0][0:1], spread[1][0:1], spread[0][1:2], spread[1][1:2],
            jnp.zeros((2, n), F32),
        ],
        axis=0,
    )
    row_ref[...] = table
    wide = jnp.concatenate([table, jnp.zeros((120, n), F32)], axis=0)
    col_ref[...] = wide.T


def kernel(
    planes, modes, orders_ref, spots_ref, mask_ref, out_ref,
    code, cosm, sinm, g_re, g_im, x_buf, w_buf, y_buf, left, right, row_tab, col_tab,
    grad, in_a, sum_a, in_b, piece, in_c, final,
    mz_s, mz_r, ml_s, ml_r, mc_s, mc_r, a_s, a_r, b_s, b_r, c_s, c_r, d_s, d_r, e_s, e_r,
):
    n = mask_ref.shape[-1]
    h = n // 2
    chips = modes // 2
    rows = n // chips
    p = lax.axis_index("plane")
    m = lax.axis_index("mode")
    core = m % 2
    chip = m // 2
    partner = m + 1 - 2 * core

    def at_chip(step):
        return (chip + step) % chips

    def rows_of(which):
        return pl.ds(pl.multiple_of(which * rows, rows), rows)

    def remote(src, dst, send, recv, plane=None, mode=None):
        return pltpu.make_async_remote_copy(
            src_ref=src, dst_ref=dst, send_sem=send, recv_sem=recv,
            device_id=(p if plane is None else plane, m if mode is None else mode),
            device_id_type=MESH,
        )

    mine = rows_of(chip)

    def mask_z(step):
        spot = code.at[p, core, mine]
        return remote(spot, spot, mz_s.at[step - 1], mz_r.at[p], plane=(p + step) % planes)

    def mask_z_in(k):
        spot = code.at[k, core, mine]
        return remote(spot, spot, mz_s.at[0], mz_r.at[k], plane=(p + 1) % planes)

    def mask_layer(k, step):
        spot = code.at[k, core, mine]
        return remote(
            spot, spot, ml_s.at[k, step - 1], ml_r.at[k, step - 1], mode=at_chip(step) * 2 + core
        )

    def mask_core(k):
        return remote(code.at[k, core], code.at[k, core], mc_s.at[k], mc_r.at[k], mode=partner)

    parts = in_b.shape[2]
    size = rows // parts

    def part_rows(which, q):
        return pl.ds(pl.multiple_of(q * (n // parts) + which * size, size), size)

    def half_rows(q):
        return pl.ds(q * (n // parts), n // parts)

    def grad_a(k, q):
        return remote(
            grad.at[k, 1 - core, half_rows(q)], in_a.at[k, half_rows(q)],
            a_s.at[k, q], a_r.at[k, q], mode=partner,
        )

    def grad_b(k, q, step):
        there = at_chip(step)
        return remote(
            sum_a.at[k, part_rows(there, q)], in_b.at[k, step - 1, q], b_s.at[k, q, step - 1],
            b_r.at[k, q, step - 1], mode=there * 2 + core,
        )

    def grad_c(k, q):
        return remote(piece.at[k, q], in_c.at[p, q], c_s.at[k, q], c_r.at[p, q], plane=k)

    def grad_c_in(source, q):
        return remote(
            piece.at[0, q], in_c.at[source, q], c_s.at[0, q], c_r.at[source, q], plane=source
        )

    def grad_d(q, step):
        spot = final.at[core, part_rows(chip, q)]
        return remote(
            spot, spot, d_s.at[q, step - 1], d_r.at[q, step - 1], mode=at_chip(step) * 2 + core
        )

    def grad_e(q, step):
        spot = final.at[core, part_rows(at_chip(chips - step), q)]
        return remote(spot, spot, e_s.at[q, step], e_r.at[q, step], mode=partner)

    barrier = pltpu.get_barrier_semaphore()
    for step in range(1, planes):
        pl.semaphore_signal(
            barrier, inc=1, device_id=((p + step) % planes, m), device_id_type=MESH
        )
    for step in range(1, chips):
        pl.semaphore_signal(
            barrier, inc=1, device_id=(p, at_chip(step) * 2 + core), device_id_type=MESH
        )
    pl.semaphore_signal(barrier, inc=1, device_id=(p, partner), device_id_type=MESH)

    def encode(half, which):
        here = rows_of(which)
        cols = pl.ds(pl.multiple_of(half * h, h), h)
        code[p, half, here] = quarter_tan(mask_ref[0, here, cols]).astype(BF16)

    encode(core, chip)
    pl.semaphore_wait(barrier, planes - 1 + chips - 1 + 1)

    for step in range(planes - 1, 0, -1):
        @pl.when((p == 0) | (p + step >= planes))
        def _():
            mask_z(step).start()

    encode(1 - core, chip)
    for step in range(1, chips):
        for half in range(2):
            encode(half, at_chip(step))
    make_operators(n, left, right)

    def spread_layer(k):
        @pl.when(p != k)
        def _():
            mask_z_in(k).wait_recv()
            for step in range(1, chips):
                mask_layer(k, step).start()

        if k == 0:
            for step in range(planes - 1, 0, -1):
                @pl.when((p > 0) & (p + step < planes))
                def _():
                    mask_z(step).start()

    def spread_core(k):
        @pl.when(p != k)
        def _():
            for step in range(1, chips):
                mask_layer(k, step).wait_recv()
            mask_core(k).start()

        if k + 1 < planes:
            spread_layer(k + 1)

    spread_layer(0)
    make_tables(
        n, orders_ref[0, p], orders_ref[1, p], spots_ref[p], right, row_tab, col_tab
    )
    spread_core(0)

    quads = [(a, b) for a in range(2) for b in range(2)]

    def span(i, a):
        return pl.ds(pl.multiple_of(a * h + i * CHUNK, CHUNK), CHUNK)

    def hadamard(q):
        top, bottom = q[0, 0] + q[0, 1], q[1, 0] + q[1, 1]
        top_d, bottom_d = q[0, 0] - q[0, 1], q[1, 0] - q[1, 1]
        return {
            (0, 0): top + bottom, (0, 1): top_d + bottom_d,
            (1, 0): top - bottom, (1, 1): top_d - bottom_d,
        }

    strips = [slice(at, at + STRIP) for at in range(0, h, STRIP)]

    def columns(strip, b):
        return slice(b * h + strip.start, b * h + strip.stop)

    def combined(i, strip):
        re = hadamard({(a, b): y_buf[b, span(i, a), columns(strip, 0)] for a, b in quads})
        im = hadamard({(a, b): y_buf[b, span(i, a), columns(strip, 1)] for a, b in quads})
        return re, im

    def put_sums(i, strip, re, im):
        for part, q in enumerate((hadamard(re), hadamard(im))):
            for a, b in quads:
                x_buf[a, span(i, part), columns(strip, b)] = q[a, b].astype(BF16)

    def products(first, second, between=None):
        for a in range(2):
            v = jnp.dot(first[a], x_buf[a], preferred_element_type=F32)
            for b in range(2):
                for part in range(2):
                    w_buf[b, a * h : (a + 1) * h, part * h : (part + 1) * h] = v[
                        part * h : (part + 1) * h, b * h : (b + 1) * h
                    ].astype(BF16)
        if between is not None:
            between()
        for b in range(2):
            y_buf[b] = jnp.dot(w_buf[b], second[b], preferred_element_type=F32)

    def outer(i, strip, a, b):
        ar, ai = col_tab[span(i, a), 2:3], col_tab[span(i, a), 3:4]
        br, bi = row_tab[4:5, columns(strip, b)], row_tab[5:6, columns(strip, b)]
        return ar * br - ai * bi, ar * bi + ai * br

    for k in range(planes):
        @pl.when(p != k)
        def _():
            mask_core(k).wait_recv()

        last = k == planes - 1

        def forward(i, carry):
            for strip in strips:
                carry = forward_strip(i, strip, carry)
            return carry

        def forward_strip(i, strip, carry):
            if k == 0:
                field_re = {
                    (a, b): col_tab[span(i, a), 0:1] * row_tab[1:2, columns(strip, b)]
                    for a, b in quads
                }
                field_im = None
            else:
                field_re, field_im = combined(i, strip)
            masked_re, masked_im = {}, {}
            for a, b in quads:
                s, c = sincos_of(code[k, b, span(i, a), strip].astype(F32))
                cosm[k, b, span(i, a), strip] = c
                sinm[k, b, span(i, a), strip] = s
                if field_im is None:
                    re, im = field_re[a, b] * c, field_re[a, b] * s
                else:
                    fr, fi = field_re[a, b], field_im[a, b]
                    re, im = fr * c - fi * s, fr * s + fi * c
                masked_re[a, b], masked_im[a, b] = re, im
                g_re[k, b, span(i, a), strip] = re.astype(BF16)
                g_im[k, b, span(i, a), strip] = im.astype(BF16)
            if not last:
                put_sums(i, strip, masked_re, masked_im)
                return carry
            total_re, total_im = carry
            for a, b in quads:
                er, ei = outer(i, strip, a, b)
                re, im = masked_re[a, b], masked_im[a, b]
                total_re += er * re - ei * im
                total_im += er * im + ei * re
            return total_re, total_im

        zero = jnp.zeros((CHUNK, STRIP), F32)
        totals = lax.fori_loop(0, h // CHUNK, forward, (zero, zero) if last else 0)
        if not last:
            products(left, right, functools.partial(spread_core, k + 1))
    coupling_re = jnp.sum(totals[0], keepdims=True)
    coupling_im = jnp.sum(totals[1], keepdims=True)

    def settle_a(k, q):
        grad_a(k, q).wait_recv()
        here = half_rows(q)
        sum_a[k, here] = (grad[k, core, here].astype(F32) + in_a[k, here].astype(F32)).astype(BF16)
        for step in range(1, chips):
            grad_b(k, q, step).start()

    def settle_b(k, q):
        for step in range(1, chips):
            grad_b(k, q, step).wait_recv()
        total = sum_a[k, part_rows(chip, q)].astype(F32)
        for step in range(1, chips):
            total += in_b[k, step - 1, q].astype(F32)
        piece[k, q] = total.astype(BF16)

        @pl.when(p != k)
        def _():
            grad_c(k, q).start()

        @pl.when(p == k)
        def _():
            in_c[k, q] = piece[k, q]

    for k in range(planes - 1, -1, -1):
        def backward(i, carry):
            for strip in strips:
                backward_strip(i, strip)
            return carry

        def backward_strip(i, strip):
            if k == planes - 1:
                back_re, back_im = {}, {}
                for a, b in quads:
                    er, ei = outer(i, strip, a, b)
                    back_re[a, b] = coupling_re * er + coupling_im * ei
                    back_im[a, b] = coupling_im * er - coupling_re * ei
            else:
                back_re, back_im = combined(i, strip)
            reply_re, reply_im = {}, {}
            for a, b in quads:
                br, bi = back_re[a, b], back_im[a, b]
                gr = g_re[k, b, span(i, a), strip].astype(F32)
                gi = g_im[k, b, span(i, a), strip].astype(F32)
                grad[k, b, span(i, a), strip] = (2.0 * (bi * gr - br * gi)).astype(BF16)
                if k > 0:
                    c, s = cosm[k, b, span(i, a), strip], sinm[k, b, span(i, a), strip]
                    reply_re[a, b] = br * c + bi * s
                    reply_im[a, b] = bi * c - br * s
            if k > 0:
                put_sums(i, strip, reply_re, reply_im)

        lax.fori_loop(0, h // CHUNK, backward, 0)
        for q in range(parts):
            grad_a(k, q).start()
        if k > 0:
            products(right, left)
        for q in range(parts):
            if k + 1 < planes:
                settle_b(k + 1, q)
        for q in range(parts):
            settle_a(k, q)
    for q in range(parts):
        settle_b(0, q)

    for q in range(parts):
        for k in range(planes):
            @pl.when(p != k)
            def _():
                grad_c_in(k, q).wait_recv()
        total = in_c[0, q].astype(F32)
        for k in range(1, planes):
            total += in_c[k, q].astype(F32)
        final[core, part_rows(chip, q)] = total.astype(BF16)
        for step in range(1, chips):
            grad_d(q, step).start()
        grad_e(q, 0).start()
    for q in range(parts):
        for step in range(1, chips):
            grad_d(q, step).wait_recv()
            grad_e(q, step).start()
    for q in range(parts):
        for step in range(chips):
            grad_e(q, step).wait_recv()

    def square(i, carry):
        here = pl.ds(pl.multiple_of(i * CHUNK, CHUNK), CHUNK)
        for b in range(2):
            g = final[b, here].astype(F32)
            carry += g * g
        return carry

    squares = lax.fori_loop(0, n // CHUNK, square, jnp.zeros((CHUNK, h), F32))
    mean_square = jnp.sum(squares, keepdims=True) * (1.0 / (n * n))
    scale = 1.0 / jnp.sqrt(mean_square + EPSILON)

    def finish(i, carry):
        here = pl.ds(pl.multiple_of(i * CHUNK, CHUNK), CHUNK)
        for b in range(2):
            cols = slice(b * h, (b + 1) * h)
            out_ref[0, here, cols] = mask_ref[0, here, cols] + final[b, here].astype(F32) * scale
        return carry

    lax.fori_loop(0, n // CHUNK, finish, 0)

    for step in range(1, planes):
        mask_z(step).wait_send()
    for k in range(planes):
        @pl.when(p != k)
        def _():
            for step in range(1, chips):
                mask_layer(k, step).wait_send()
            mask_core(k).wait_send()
            for q in range(parts):
                grad_c(k, q).wait_send()

        for q in range(parts):
            grad_a(k, q).wait_send()
            for step in range(1, chips):
                grad_b(k, q, step).wait_send()
    for q in range(parts):
        for step in range(1, chips):
            grad_d(q, step).wait_send()
        for step in range(chips):
            grad_e(q, step).wait_send()


def shards(planes, modes, phase_masks, hg_orders, spot_index):
    n = phase_masks.shape[1]
    h = n // 2
    chips = modes // 2
    rows = n // chips
    others = max(chips - 1, 1)
    parts = 2 if rows % 32 == 0 else 1
    assert hg_orders.shape[0] == planes and n & (n - 1) == 0
    dma = pltpu.SemaphoreType.DMA
    vmem = pltpu.VMEM
    return pl.pallas_call(
        functools.partial(kernel, planes, modes),
        out_shape=jax.ShapeDtypeStruct((1, n, n), F32),
        in_specs=[
            pl.BlockSpec(memory_space=pltpu.SMEM),
            pl.BlockSpec(memory_space=pltpu.SMEM),
            pl.BlockSpec(memory_space=pltpu.VMEM),
        ],
        out_specs=pl.BlockSpec(memory_space=pltpu.VMEM),
        scratch_shapes=[
            vmem((planes, 2, n, h), BF16),
            vmem((planes, 2, n, h), F32),
            vmem((planes, 2, n, h), F32),
            vmem((planes, 2, n, h), BF16),
            vmem((planes, 2, n, h), BF16),
            vmem((2, n, n), BF16),
            vmem((2, n, n), BF16),
            vmem((2, n, n), F32),
            vmem((2, n, n), BF16),
            vmem((2, n, n), BF16),
            vmem((8, n), F32),
            vmem((n, 128), F32),
            vmem((planes, 2, n, h), BF16),
            vmem((planes, n, h), BF16),
            vmem((planes, n, h), BF16),
            vmem((planes, others, parts, rows // parts, h), BF16),
            vmem((planes, parts, rows // parts, h), BF16),
            vmem((planes, parts, rows // parts, h), BF16),
            vmem((2, n, h), BF16),
            dma((max(planes - 1, 1),)), dma((planes,)),
            dma((planes, others)), dma((planes, others)),
            dma((planes,)), dma((planes,)),
            dma((planes, parts)), dma((planes, parts)),
            dma((planes, parts, others)), dma((planes, parts, others)),
            dma((planes, parts)), dma((planes, parts)),
            dma((parts, others)), dma((parts, others)),
            dma((parts, chips)), dma((parts, chips)),
        ],
        compiler_params=pltpu.CompilerParams(
            collective_id=0, has_side_effects=True, vmem_limit_bytes=52 * 1024 * 1024
        ),
        name="phase_update",
    )(hg_orders.T, spot_index, phase_masks)


def solution(mesh):
    planes, modes = mesh.shape["plane"], mesh.shape["mode"]
    return jax.shard_map(
        functools.partial(shards, planes, modes),
        mesh=mesh,
        in_specs=(P("plane", None, None), P("mode", None), P("mode")),
        out_specs=P("plane", None, None),
        check_vma=False,
    )
```

```python
import functools
import math

import jax
import jax.numpy as jnp
from jax import lax
from jax.experimental import pallas as pl
from jax.experimental.pallas import tpu as pltpu
from jax.sharding import PartitionSpec as P

ORDERS = 45
SPOT_SIDE = 32
CHIRP_RATE = math.pi / 48.0 * (math.pi / 48.0)
AMPLITUDE = 12.0
EPSILON = 1e-06
CHUNK = 16
STRIP = 128
F32 = jnp.float32
BF16 = jnp.bfloat16
MESH = pl.DeviceIdType.MESH

SIN_HALF = [(-1.0) ** n / math.factorial(2 * n + 1) for n in range(6)]
COS_HALF = [(-1.0) ** n / math.factorial(2 * n) for n in range(6)]


def horner(u, coefficients):
    total = jnp.full_like(u, coefficients[-1])
    for value in coefficients[-2::-1]:
        total = total * u + value
    return total


def sincos(x):
    h = 0.5 * x
    u = h * h
    s = h * horner(u, SIN_HALF)
    c = horner(u, COS_HALF)
    return 2.0 * s * c, 1.0 - 2.0 * s * s


def quarter_tan(x):
    h = 0.5 * x
    u = h * h
    return h * horner(u, SIN_HALF) / (1.0 + horner(u, COS_HALF))


def sincos_of(t):
    twice = 2.0 / (1.0 + t * t)
    half_cos = twice - 1.0
    half_sin = t * twice
    double = 2.0 * half_sin
    return double * half_cos, 1.0 - double * half_sin


def split(x):
    high = x.astype(BF16)
    return high, (x - high.astype(F32)).astype(BF16)


def make_operators(n, left_ref, right_ref):
    h = n // 2
    rows = lax.broadcasted_iota(jnp.int32, (h, h), 0)
    slots = lax.broadcasted_iota(jnp.int32, (h, h), 1)
    for a in range(2):
        freq = 2 * slots + a
        turn = ((freq * rows + h) & (n - 1)) - h
        s, c = sincos(turn.astype(F32) * (2.0 * math.pi / n))
        basis = jnp.concatenate([c, s], axis=1)
        freq_row = 2 * lax.broadcasted_iota(jnp.int32, (8, h), 1) + a
        centred = ((freq_row + h) & (n - 1)) - h
        turns = (centred * centred).astype(F32) * (CHIRP_RATE / (2.0 * math.pi))
        turns = turns - jnp.floor(turns + 0.5)
        chirp_s, chirp_c = sincos(turns * (2.0 * math.pi))
        weighted = []
        for weight in (chirp_c, -chirp_s):
            weight = weight[:1] * (1.0 / n)
            weighted.append(basis * jnp.concatenate([weight, weight], axis=1))
        high, low = split(jnp.concatenate(weighted, axis=0))
        basis_high, basis_low = split(basis)
        prop = lax.dot_general(
            jnp.concatenate([high, high, low], axis=1),
            jnp.concatenate([basis_high, basis_low, basis_high], axis=1),
            (((1,), (1,)), ((), ())), preferred_element_type=F32,
        ).astype(BF16)
        re, im = prop[:h], prop[h:]
        left_ref[a, :h, :h] = re
        left_ref[a, :h, h:] = -im
        left_ref[a, h:, :h] = im
        left_ref[a, h:, h:] = re
        right_ref[a, :h, :h] = re
        right_ref[a, :h, h:] = im
        right_ref[a, h:, :h] = -im
        right_ref[a, h:, h:] = re


def make_tables(n, order_x, order_y, spot, right_ref, row_ref, col_ref):
    h = n // 2
    coords = lax.broadcasted_iota(jnp.int32, (8, n), 1).astype(F32) - (n - 1) / 2.0
    row_id = lax.broadcasted_iota(jnp.int32, (8, n), 0)
    orders = jnp.where(row_id == 0, order_x, order_y)
    scaled = coords * (48.0 / n)
    previous = math.pow(math.pi, -0.25) * jnp.exp(-0.5 * scaled * scaled)
    current = math.sqrt(2.0) * scaled * previous
    picked = jnp.where(orders == 0, previous, current)
    for degree in range(1, ORDERS - 1):
        higher = (
            math.sqrt(2.0 / (degree + 1.0)) * scaled * current
            - math.sqrt(degree / (degree + 1.0)) * previous
        )
        picked = jnp.where(orders == degree + 1, higher, picked)
        previous, current = current, higher
    centre = (SPOT_SIDE - 1) / 2.0
    spot_row = (spot // SPOT_SIDE).astype(F32) - centre
    spot_col = (spot % SPOT_SIDE).astype(F32) - centre
    place = jnp.where(row_id == 0, spot_row, spot_col)
    offset = (coords - (n / 40.0) * place) * (120.0 / n)
    profile = jnp.exp(-offset * offset)
    halves = []
    for a, folded in enumerate(
        (profile[:, :h] + profile[:, h:], profile[:, :h] - profile[:, h:])
    ):
        high, low = split(folded)
        both = jnp.dot(
            jnp.concatenate([high, low], axis=0), right_ref[a, :h], preferred_element_type=F32
        )
        halves.append(both[:8] + both[8:])
    spread = []
    for part in range(2):
        s, d = (half[:, part * h : (part + 1) * h] for half in halves)
        spread.append(jnp.concatenate([s + d, s - d], axis=1))
    table = jnp.concatenate(
        [
            AMPLITUDE * picked[0:1], picked[1:2],
            spread[0][0:1], spread[1][0:1], spread[0][1:2], spread[1][1:2],
            jnp.zeros((2, n), F32),
        ],
        axis=0,
    )
    row_ref[...] = table
    wide = jnp.concatenate([table, jnp.zeros((120, n), F32)], axis=0)
    col_ref[...] = wide.T


def kernel(
    planes, modes, orders_ref, spots_ref, mask_ref, out_ref,
    code, cosm, sinm, g_re, g_im, x_buf, w_buf, y_buf, left, right, row_tab, col_tab,
    grad, in_a, sum_a, in_b, piece, in_c, final,
    mz_s, mz_r, ml_s, ml_r, mc_s, mc_r, a_s, a_r, b_s, b_r, c_s, c_r, d_s, d_r, e_s, e_r,
):
    n = mask_ref.shape[-1]
    h = n // 2
    chips = modes // 2
    rows = n // chips
    p = lax.axis_index("plane")
    m = lax.axis_index("mode")
    core = m % 2
    chip = m // 2
    partner = m + 1 - 2 * core

    def at_chip(step):
        return (chip + step) % chips

    def rows_of(which):
        return pl.ds(pl.multiple_of(which * rows, rows), rows)

    def remote(src, dst, send, recv, plane=None, mode=None):
        return pltpu.make_async_remote_copy(
            src_ref=src, dst_ref=dst, send_sem=send, recv_sem=recv,
            device_id=(p if plane is None else plane, m if mode is None else mode),
            device_id_type=MESH,
        )

    mine = rows_of(chip)

    def mask_z(step):
        spot = code.at[p, core, mine]
        return remote(spot, spot, mz_s.at[step - 1], mz_r.at[p], plane=(p + step) % planes)

    def mask_z_in(k):
        spot = code.at[k, core, mine]
        return remote(spot, spot, mz_s.at[0], mz_r.at[k], plane=(p + 1) % planes)

    def mask_layer(k, step):
        spot = code.at[k, core, mine]
        return remote(
            spot, spot, ml_s.at[k, step - 1], ml_r.at[k, step - 1], mode=at_chip(step) * 2 + core
        )

    def mask_core(k):
        return remote(code.at[k, core], code.at[k, core], mc_s.at[k], mc_r.at[k], mode=partner)

    parts = in_b.shape[2]
    size = rows // parts

    def part_rows(which, q):
        return pl.ds(pl.multiple_of(q * (n // parts) + which * size, size), size)

    def half_rows(q):
        return pl.ds(q * (n // parts), n // parts)

    def grad_a(k, q):
        return remote(
            grad.at[k, 1 - core, half_rows(q)], in_a.at[k, half_rows(q)],
            a_s.at[k, q], a_r.at[k, q], mode=partner,
        )

    def grad_b(k, q, step):
        there = at_chip(step)
        return remote(
            sum_a.at[k, part_rows(there, q)], in_b.at[k, step - 1, q], b_s.at[k, q, step - 1],
            b_r.at[k, q, step - 1], mode=there * 2 + core,
        )

    def grad_c(k, q):
        return remote(piece.at[k, q], in_c.at[p, q], c_s.at[k, q], c_r.at[p, q], plane=k)

    def grad_c_in(source, q):
        return remote(
            piece.at[0, q], in_c.at[source, q], c_s.at[0, q], c_r.at[source, q], plane=source
        )

    def grad_d(q, step):
        spot = final.at[core, part_rows(chip, q)]
        return remote(
            spot, spot, d_s.at[q, step - 1], d_r.at[q, step - 1], mode=at_chip(step) * 2 + core
        )

    def grad_e(q, step):
        spot = final.at[core, part_rows(at_chip(chips - step), q)]
        return remote(spot, spot, e_s.at[q, step], e_r.at[q, step], mode=partner)

    barrier = pltpu.get_barrier_semaphore()
    for step in range(1, planes):
        pl.semaphore_signal(
            barrier, inc=1, device_id=((p + step) % planes, m), device_id_type=MESH
        )
    for step in range(1, chips):
        pl.semaphore_signal(
            barrier, inc=1, device_id=(p, at_chip(step) * 2 + core), device_id_type=MESH
        )
    pl.semaphore_signal(barrier, inc=1, device_id=(p, partner), device_id_type=MESH)

    def encode(half, which):
        here = rows_of(which)
        cols = pl.ds(pl.multiple_of(half * h, h), h)
        code[p, half, here] = quarter_tan(mask_ref[0, here, cols]).astype(BF16)

    encode(core, chip)
    pl.semaphore_wait(barrier, planes - 1 + chips - 1 + 1)

    for step in range(planes - 1, 0, -1):
        mask_z(step).start()

    encode(1 - core, chip)
    for step in range(1, chips):
        for half in range(2):
            encode(half, at_chip(step))
    make_operators(n, left, right)

    def spread_layer(k):
        @pl.when(p != k)
        def _():
            mask_z_in(k).wait_recv()
            for step in range(1, chips):
                mask_layer(k, step).start()

    def spread_core(k):
        @pl.when(p != k)
        def _():
            for step in range(1, chips):
                mask_layer(k, step).wait_recv()
            mask_core(k).start()

    for k in range(min(2, planes)):
        spread_layer(k)

    make_tables(
        n, orders_ref[0, p], orders_ref[1, p], spots_ref[p], right, row_tab, col_tab
    )
    for k in range(2, planes):
        spread_layer(k)
    spread_core(0)

    quads = [(a, b) for a in range(2) for b in range(2)]

    def span(i, a):
        return pl.ds(pl.multiple_of(a * h + i * CHUNK, CHUNK), CHUNK)

    def hadamard(q):
        top, bottom = q[0, 0] + q[0, 1], q[1, 0] + q[1, 1]
        top_d, bottom_d = q[0, 0] - q[0, 1], q[1, 0] - q[1, 1]
        return {
            (0, 0): top + bottom, (0, 1): top_d + bottom_d,
            (1, 0): top - bottom, (1, 1): top_d - bottom_d,
        }

    strips = [slice(at, at + STRIP) for at in range(0, h, STRIP)]

    def columns(strip, b):
        return slice(b * h + strip.start, b * h + strip.stop)

    def combined(i, strip):
        re = hadamard({(a, b): y_buf[b, span(i, a), columns(strip, 0)] for a, b in quads})
        im = hadamard({(a, b): y_buf[b, span(i, a), columns(strip, 1)] for a, b in quads})
        return re, im

    def put_sums(i, strip, re, im):
        for part, q in enumerate((hadamard(re), hadamard(im))):
            for a, b in quads:
                x_buf[a, span(i, part), columns(strip, b)] = q[a, b].astype(BF16)

    def products(first, second):
        for a in range(2):
            v = jnp.dot(first[a], x_buf[a], preferred_element_type=F32)
            for b in range(2):
                for part in range(2):
                    w_buf[b, a * h : (a + 1) * h, part * h : (part + 1) * h] = v[
                        part * h : (part + 1) * h, b * h : (b + 1) * h
                    ].astype(BF16)
        for b in range(2):
            y_buf[b] = jnp.dot(w_buf[b], second[b], preferred_element_type=F32)

    def outer(i, strip, a, b):
        ar, ai = col_tab[span(i, a), 2:3], col_tab[span(i, a), 3:4]
        br, bi = row_tab[4:5, columns(strip, b)], row_tab[5:6, columns(strip, b)]
        return ar * br - ai * bi, ar * bi + ai * br

    for k in range(planes):
        @pl.when(p != k)
        def _():
            mask_core(k).wait_recv()

        last = k == planes - 1

        def forward(i, carry):
            for strip in strips:
                carry = forward_strip(i, strip, carry)
            return carry

        def forward_strip(i, strip, carry):
            if k == 0:
                field_re = {
                    (a, b): col_tab[span(i, a), 0:1] * row_tab[1:2, columns(strip, b)]
                    for a, b in quads
                }
                field_im = None
            else:
                field_re, field_im = combined(i, strip)
            masked_re, masked_im = {}, {}
            for a, b in quads:
                s, c = sincos_of(code[k, b, span(i, a), strip].astype(F32))
                cosm[k, b, span(i, a), strip] = c
                sinm[k, b, span(i, a), strip] = s
                if field_im is None:
                    re, im = field_re[a, b] * c, field_re[a, b] * s
                else:
                    fr, fi = field_re[a, b], field_im[a, b]
                    re, im = fr * c - fi * s, fr * s + fi * c
                masked_re[a, b], masked_im[a, b] = re, im
                g_re[k, b, span(i, a), strip] = re.astype(BF16)
                g_im[k, b, span(i, a), strip] = im.astype(BF16)
            if not last:
                put_sums(i, strip, masked_re, masked_im)
                return carry
            total_re, total_im = carry
            for a, b in quads:
                er, ei = outer(i, strip, a, b)
                re, im = masked_re[a, b], masked_im[a, b]
                total_re += er * re - ei * im
                total_im += er * im + ei * re
            return total_re, total_im

        zero = jnp.zeros((CHUNK, STRIP), F32)
        totals = lax.fori_loop(0, h // CHUNK, forward, (zero, zero) if last else 0)
        if not last:
            spread_core(k + 1)
            products(left, right)
    coupling_re = jnp.sum(totals[0], keepdims=True)
    coupling_im = jnp.sum(totals[1], keepdims=True)

    def settle_a(k, q):
        grad_a(k, q).wait_recv()
        here = half_rows(q)
        sum_a[k, here] = (grad[k, core, here].astype(F32) + in_a[k, here].astype(F32)).astype(BF16)
        for step in range(1, chips):
            grad_b(k, q, step).start()

    def settle_b(k, q):
        for step in range(1, chips):
            grad_b(k, q, step).wait_recv()
        total = sum_a[k, part_rows(chip, q)].astype(F32)
        for step in range(1, chips):
            total += in_b[k, step - 1, q].astype(F32)
        piece[k, q] = total.astype(BF16)

        @pl.when(p != k)
        def _():
            grad_c(k, q).start()

        @pl.when(p == k)
        def _():
            in_c[k, q] = piece[k, q]

    for k in range(planes - 1, -1, -1):
        def backward(i, carry):
            for strip in strips:
                backward_strip(i, strip)
            return carry

        def backward_strip(i, strip):
            if k == planes - 1:
                back_re, back_im = {}, {}
                for a, b in quads:
                    er, ei = outer(i, strip, a, b)
                    back_re[a, b] = coupling_re * er + coupling_im * ei
                    back_im[a, b] = coupling_im * er - coupling_re * ei
            else:
                back_re, back_im = combined(i, strip)
            reply_re, reply_im = {}, {}
            for a, b in quads:
                br, bi = back_re[a, b], back_im[a, b]
                gr = g_re[k, b, span(i, a), strip].astype(F32)
                gi = g_im[k, b, span(i, a), strip].astype(F32)
                grad[k, b, span(i, a), strip] = (2.0 * (bi * gr - br * gi)).astype(BF16)
                if k > 0:
                    c, s = cosm[k, b, span(i, a), strip], sinm[k, b, span(i, a), strip]
                    reply_re[a, b] = br * c + bi * s
                    reply_im[a, b] = bi * c - br * s
            if k > 0:
                put_sums(i, strip, reply_re, reply_im)

        lax.fori_loop(0, h // CHUNK, backward, 0)
        for q in range(parts):
            grad_a(k, q).start()
        if k > 0:
            products(right, left)
        for q in range(parts):
            if k + 1 < planes:
                settle_b(k + 1, q)
        for q in range(parts):
            settle_a(k, q)
    for q in range(parts):
        settle_b(0, q)

    for q in range(parts):
        for k in range(planes):
            @pl.when(p != k)
            def _():
                grad_c_in(k, q).wait_recv()
        total = in_c[0, q].astype(F32)
        for k in range(1, planes):
            total += in_c[k, q].astype(F32)
        final[core, part_rows(chip, q)] = total.astype(BF16)
        for step in range(1, chips):
            grad_d(q, step).start()
        grad_e(q, 0).start()
    for q in range(parts):
        for step in range(1, chips):
            grad_d(q, step).wait_recv()
            grad_e(q, step).start()
    for q in range(parts):
        for step in range(chips):
            grad_e(q, step).wait_recv()

    def square(i, carry):
        here = pl.ds(pl.multiple_of(i * CHUNK, CHUNK), CHUNK)
        for b in range(2):
            g = final[b, here].astype(F32)
            carry += g * g
        return carry

    squares = lax.fori_loop(0, n // CHUNK, square, jnp.zeros((CHUNK, h), F32))
    mean_square = jnp.sum(squares, keepdims=True) * (1.0 / (n * n))
    scale = 1.0 / jnp.sqrt(mean_square + EPSILON)

    def finish(i, carry):
        here = pl.ds(pl.multiple_of(i * CHUNK, CHUNK), CHUNK)
        for b in range(2):
            cols = slice(b * h, (b + 1) * h)
            out_ref[0, here, cols] = mask_ref[0, here, cols] + final[b, here].astype(F32) * scale
        return carry

    lax.fori_loop(0, n // CHUNK, finish, 0)

    for step in range(1, planes):
        mask_z(step).wait_send()
    for k in range(planes):
        @pl.when(p != k)
        def _():
            for step in range(1, chips):
                mask_layer(k, step).wait_send()
            mask_core(k).wait_send()
            for q in range(parts):
                grad_c(k, q).wait_send()

        for q in range(parts):
            grad_a(k, q).wait_send()
            for step in range(1, chips):
                grad_b(k, q, step).wait_send()
    for q in range(parts):
        for step in range(1, chips):
            grad_d(q, step).wait_send()
        for step in range(chips):
            grad_e(q, step).wait_send()


def shards(planes, modes, phase_masks, hg_orders, spot_index):
    n = phase_masks.shape[1]
    h = n // 2
    chips = modes // 2
    rows = n // chips
    others = max(chips - 1, 1)
    parts = 2 if rows % 32 == 0 else 1
    assert hg_orders.shape[0] == planes and n & (n - 1) == 0
    dma = pltpu.SemaphoreType.DMA
    vmem = pltpu.VMEM
    return pl.pallas_call(
        functools.partial(kernel, planes, modes),
        out_shape=jax.ShapeDtypeStruct((1, n, n), F32),
        in_specs=[
            pl.BlockSpec(memory_space=pltpu.SMEM),
            pl.BlockSpec(memory_space=pltpu.SMEM),
            pl.BlockSpec(memory_space=pltpu.VMEM),
        ],
        out_specs=pl.BlockSpec(memory_space=pltpu.VMEM),
        scratch_shapes=[
            vmem((planes, 2, n, h), BF16),
            vmem((planes, 2, n, h), F32),
            vmem((planes, 2, n, h), F32),
            vmem((planes, 2, n, h), BF16),
            vmem((planes, 2, n, h), BF16),
            vmem((2, n, n), BF16),
            vmem((2, n, n), BF16),
            vmem((2, n, n), F32),
            vmem((2, n, n), BF16),
            vmem((2, n, n), BF16),
            vmem((8, n), F32),
            vmem((n, 128), F32),
            vmem((planes, 2, n, h), BF16),
            vmem((planes, n, h), BF16),
            vmem((planes, n, h), BF16),
            vmem((planes, others, parts, rows // parts, h), BF16),
            vmem((planes, parts, rows // parts, h), BF16),
            vmem((planes, parts, rows // parts, h), BF16),
            vmem((2, n, h), BF16),
            dma((max(planes - 1, 1),)), dma((planes,)),
            dma((planes, others)), dma((planes, others)),
            dma((planes,)), dma((planes,)),
            dma((planes, parts)), dma((planes, parts)),
            dma((planes, parts, others)), dma((planes, parts, others)),
            dma((planes, parts)), dma((planes, parts)),
            dma((parts, others)), dma((parts, others)),
            dma((parts, chips)), dma((parts, chips)),
        ],
        compiler_params=pltpu.CompilerParams(
            collective_id=0, has_side_effects=True, vmem_limit_bytes=52 * 1024 * 1024
        ),
        name="phase_update",
    )(hg_orders.T, spot_index, phase_masks)


def solution(mesh):
    planes, modes = mesh.shape["plane"], mesh.shape["mode"]
    return jax.shard_map(
        functools.partial(shards, planes, modes),
        mesh=mesh,
        in_specs=(P("plane", None, None), P("mode", None), P("mode")),
        out_specs=P("plane", None, None),
        check_vma=False,
    )
```
